512 devices in a mesh: dp: 16 (over x_hi, y, core), space: 32 (over z, x_lo).
Axes of the slice: x: 4 (x_hi: 2, x_lo: 2; x = x_hi * 2 + x_lo), y: 4, z: 16, core: 2. Of those that a mesh axis runs over, the one named last changes fastest.
Arguments:
- fields: bfloat16 [16, 32, 48, 48, 128], P('dp', 'space'), may hold values from -6 to 6
- cotangent: bfloat16 [16, 32, 48, 48, 128], P('dp', 'space'), may hold values from -6 to 6
- land_mask: int32 [32, 48, 48], P('space'), may hold values from 0 to 1, as said below
- neighbours: int32 [32, 8], P('space'), may hold values from -1 to 31, as said below
- conv_kernel: float32 [7, 7, 128], replicated, may hold values from -0.875 to 0.875
- norm_gain: float32 [128], replicated, may hold values from 0.25 to 1.75
- up_weight: bfloat16 [128, 512], replicated, may hold values from -0.5 to 0.5
- up_bias: float32 [512], replicated, may hold values from -3 to 3
- down_weight: bfloat16 [512, 128], replicated, may hold values from -0.25 to 0.25
- layer_scale: float32 [128], replicated, may hold values from 0.3 to 1.5
Outputs:
- block_out: bfloat16 [16, 32, 48, 48, 128], P('dp', 'space')
- fields_grad: bfloat16 [16, 32, 48, 48, 128], P('dp', 'space')
- kernel_grad: float32 [7, 7, 128], replicated
- gain_grad: float32 [128], replicated
- up_weight_grad: float32 [128, 512], replicated
- up_bias_grad: float32 [512], replicated
- down_weight_grad: float32 [512, 128], replicated
- scale_grad: float32 [128], replicated
The draws below stay inside these ranges and needn't reach their ends.
Inputs may be any that keep to these rules, and one draw needn't show every extreme that they name: `neighbours`: row t gives the ids of the tiles beside tile t in the order north, south, west, east, north-west, north-east, south-west, south-east, or -1. The curve runs over 32 + 8 tile positions in rows of two, alternately west to east and east to west, from the northern row southwards; 8 positions are land and skipped, and the 32 wet tiles are numbered along it, one in every slot. The relation is symmetric; a west or east neighbour differs from t by exactly 1, a northern one is lower and a southern one higher, and the difference reaches 3 and never more. `land_mask`: 1 for a sea cell, 0 for land; every tile has sea cells.
All inputs are finite; a program needn't handle non-finite values.
Results may differ from the reference program's by a relative error of at most 0.007.
Values may be sent and summed in bfloat16 or wider, within the bound.
No kernel may reach another device: no remote copies, remote signals or barrier semaphores. Data moves between devices by JAX's collectives and lax.ppermute only.
A program may use at most 64 MiB of HBM per device.

```python
import math
import jax
import jax.numpy as jnp
from jax import lax

C = 128
HID = 512
KERNEL = 7
DILATION = 2
TILE = 48
HALO = 6
MEMBERS = 16
TILES = 32
LAND_TILES = 8
CELLS = 1179648


def curve_layout(key):
    spots = TILES + LAND_TILES
    which_end = jax.random.randint(jax.random.fold_in(key, 11), (), 0, 2).astype(jnp.int32)
    shuffled = jax.random.permutation(key, spots - 4).astype(jnp.int32) + 4 * which_end
    dropped = shuffled[:LAND_TILES]
    positions = jnp.arange(spots, dtype=jnp.int32)
    is_land = jnp.any(positions[:, None] == dropped[None, :], axis=1)
    wet_flag = jnp.where(is_land, 0, 1).astype(jnp.int32)
    wet_index = (jnp.cumsum(wet_flag) - 1).astype(jnp.int32)
    slot_position = jnp.argsort(is_land.astype(jnp.int32) * spots + positions).astype(jnp.int32)[:TILES]
    return (wet_flag, wet_index, slot_position)


def draw_neighbours(key, part):
    wet_flag, wet_index, slot_position = curve_layout(key)
    spots = TILES + LAND_TILES
    grid_row = slot_position // 2
    grid_col = jnp.where(grid_row % 2 == 0, slot_position % 2, 1 - slot_position % 2)
    step_row = jnp.array([-1, 1, 0, 0, -1, -1, 1, 1], jnp.int32)
    step_col = jnp.array([0, 0, -1, 1, -1, 1, -1, 1], jnp.int32)
    other_row = grid_row[:, None] + step_row[None, :]
    other_col = grid_col[:, None] + step_col[None, :]
    inside = (other_row >= 0) & (other_row < spots // 2) & (other_col >= 0) & (other_col < 2)
    other_pos = 2 * other_row + jnp.where(other_row % 2 == 0, other_col, 1 - other_col)
    clipped = jnp.clip(other_pos, 0, spots - 1)
    found = inside & (wet_flag[clipped] == 1)
    return jnp.where(found, wet_index[clipped], -1).astype(jnp.int32)


def draw_land_mask(key, part):
    key = jax.random.fold_in(key, 7)
    land_level = jax.random.randint(jax.random.fold_in(key, 1), (TILES, 1, 1), 0, 5)
    cell_draw = jax.random.randint(jax.random.fold_in(key, 2), (TILES, TILE, TILE), 0, 8)
    return jnp.where(cell_draw >= land_level, 1, 0).astype(jnp.int32)


def shard_levels(stream_key, extent, cuts, smallest, largest):
    gain = 1.0
    for position, parts in cuts:
        draws = jax.random.uniform(jax.random.fold_in(jax.random.fold_in(stream_key, 6), position), (parts,), jnp.float32, smallest / len(cuts), largest / len(cuts))
        gain = gain * jnp.repeat(jnp.exp(draws), extent[position] // parts).reshape((-1,) + (1,) * (len(extent) - 1 - position))
    return gain


def bell_draw(stream_key, shape, deviation, most, shards=(), kind=jnp.bfloat16):
    loudness = shard_levels(stream_key, shape, shards, -0.22, 0.18) if shards else 1.0
    entries = jax.random.normal(stream_key, shape, jnp.float32) * deviation * loudness
    return jnp.minimum(jnp.maximum(entries, -most), most).astype(kind)


def setup_inputs(seed: int = 0) -> dict:
    key_of = jax.random.split(jax.random.key(seed), 11)
    fields = bell_draw(key_of[0], (MEMBERS, TILES, TILE, TILE, C), 1.0, 6.0, ((0, 16), (1, 32)))
    cotangent = bell_draw(key_of[1], (MEMBERS, TILES, TILE, TILE, C), 1.0, 6.0, ((0, 16), (1, 32)))
    land_mask = draw_land_mask(jax.random.fold_in(key_of[10], 71), 0)
    neighbours = draw_neighbours(jax.random.fold_in(key_of[10], 71), 0)
    conv_kernel = bell_draw(key_of[4], (KERNEL, KERNEL, C), (KERNEL * KERNEL) ** -0.5, 0.875, (), jnp.float32)
    norm_gain = jnp.clip(1.0 + 0.15 * jax.random.normal(key_of[5], (C,), jnp.float32), 0.25, 1.75)
    up_weight = bell_draw(key_of[6], (C, HID), C ** -0.5, 0.5)
    up_bias = bell_draw(key_of[7], (HID,), 0.5, 3.0, (), jnp.float32)
    down_weight = bell_draw(key_of[8], (HID, C), HID ** -0.5, 0.25)
    layer_scale = jnp.clip(jnp.exp(jax.random.uniform(key_of[9], (C,), jnp.float32, math.log(0.3), math.log(1.5))), 0.3, 1.5)
    return dict(fields=fields, cotangent=cotangent, land_mask=land_mask, neighbours=neighbours, conv_kernel=conv_kernel, norm_gain=norm_gain, up_weight=up_weight, up_bias=up_bias, down_weight=down_weight, layer_scale=layer_scale)


norm_eps = 1e-06
inv_sqrt_two = 0.7071067811865476
inv_sqrt_two_pi = 0.3989422804014327

def extend_tiles(tile_data, neighbours):
    top_rows = tile_data[:, :HALO]
    bottom_rows = tile_data[:, -HALO:]
    left_columns = tile_data[:, :, :HALO]
    right_columns = tile_data[:, :, -HALO:]

    def choose_strip(band, direction):
        source = neighbours[:, direction]
        strip = jnp.take(band, jnp.maximum(source, 0), axis=0)
        return jnp.where((source >= 0)[:, None, None, None], strip, jnp.zeros_like(strip))
    north = choose_strip(bottom_rows, 0)
    south = choose_strip(top_rows, 1)
    west = choose_strip(right_columns, 2)
    east = choose_strip(left_columns, 3)
    north_west = choose_strip(bottom_rows, 4)[:, :, -HALO:]
    north_east = choose_strip(bottom_rows, 5)[:, :, :HALO]
    south_west = choose_strip(top_rows, 6)[:, :, -HALO:]
    south_east = choose_strip(top_rows, 7)[:, :, :HALO]
    upper = jnp.concatenate([north_west, north, north_east], axis=2)
    middle = jnp.concatenate([west, tile_data, east], axis=2)
    lower = jnp.concatenate([south_west, south, south_east], axis=2)
    return jnp.concatenate([upper, middle, lower], axis=1)

def depthwise(extended, conv_kernel):
    tile_rows = extended.shape[-3] - 2 * HALO
    tile_cols = extended.shape[-2] - 2 * HALO
    running = jnp.zeros(extended.shape[:-3] + (tile_rows, tile_cols, extended.shape[-1]), jnp.float32)
    for tap_row in range(KERNEL):
        for tap_col in range(KERNEL):
            window = extended[..., DILATION * tap_row:DILATION * tap_row + tile_rows, DILATION * tap_col:DILATION * tap_col + tile_cols, :]
            running = running + conv_kernel[tap_row, tap_col] * window.astype(jnp.float32)
    return running

def depthwise_transpose(grad_extended, conv_kernel):
    tile_rows = grad_extended.shape[-3] - 2 * HALO
    tile_cols = grad_extended.shape[-2] - 2 * HALO
    running = jnp.zeros(grad_extended.shape[:-3] + (tile_rows, tile_cols, grad_extended.shape[-1]), jnp.float32)
    for tap_row in range(KERNEL):
        for tap_col in range(KERNEL):
            row_start = 2 * HALO - DILATION * tap_row
            col_start = 2 * HALO - DILATION * tap_col
            window = grad_extended[..., row_start:row_start + tile_rows, col_start:col_start + tile_cols, :]
            running = running + conv_kernel[tap_row, tap_col] * window.astype(jnp.float32)
    return running

def kernel_sums(conv_grad, extended):
    tile_rows = conv_grad.shape[-3]
    tile_cols = conv_grad.shape[-2]
    upstream = conv_grad.astype(jnp.float32)
    lead_axes = tuple(range(conv_grad.ndim - 1))
    rows_out = []
    for tap_row in range(KERNEL):
        row_terms = []
        for tap_col in range(KERNEL):
            window = extended[..., DILATION * tap_row:DILATION * tap_row + tile_rows, DILATION * tap_col:DILATION * tap_col + tile_cols, :]
            row_terms.append(lax.optimization_barrier(jnp.sum(upstream * window.astype(jnp.float32), axis=lead_axes)))
        rows_out.append(jnp.stack(row_terms))
    return jnp.stack(rows_out)

def block_pass(fields, cotangent, maskf, extended, extend_fn, conv_kernel, norm_gain, up_weight, up_bias, down_weight, layer_scale):
    channels = fields.shape[-1]
    lead_axes = tuple(range(fields.ndim - 1))
    conv = depthwise(extended, conv_kernel)
    chan_mean = lax.optimization_barrier(jnp.mean(conv, axis=-1, keepdims=True))
    centered = conv - chan_mean
    inv_std = lax.rsqrt(lax.optimization_barrier(jnp.mean(centered * centered, axis=-1, keepdims=True)) + norm_eps)
    standard = centered * inv_std
    normed = (standard * norm_gain).astype(jnp.bfloat16).reshape(-1, channels)
    hidden = jnp.dot(normed, up_weight, preferred_element_type=jnp.float32) + up_bias
    active = jax.nn.gelu(hidden, approximate=False).astype(jnp.bfloat16)
    branch = jnp.dot(active, down_weight, preferred_element_type=jnp.float32).reshape(fields.shape)
    block_out = (fields.astype(jnp.float32) + maskf * layer_scale * branch).astype(jnp.bfloat16)
    upstream = cotangent.astype(jnp.float32)
    scale_term = lax.optimization_barrier(jnp.sum(maskf * branch * upstream, axis=lead_axes))
    branch_grad = (maskf * layer_scale * upstream).astype(jnp.bfloat16).reshape(-1, channels)
    down_term = lax.dot_general(active, branch_grad, (((0,), (0,)), ((), ())), preferred_element_type=jnp.float32)
    active_grad = lax.dot_general(branch_grad, down_weight, (((1,), (1,)), ((), ())), preferred_element_type=jnp.float32)
    gelu_slope = 0.5 * (1.0 + lax.erf(hidden * inv_sqrt_two)) + hidden * jnp.exp(-0.5 * hidden * hidden) * inv_sqrt_two_pi
    hidden_grad = (active_grad * gelu_slope).astype(jnp.bfloat16)
    up_term = lax.dot_general(normed, hidden_grad, (((0,), (0,)), ((), ())), preferred_element_type=jnp.float32)
    bias_term = lax.optimization_barrier(jnp.sum(hidden_grad.astype(jnp.float32), axis=0))
    normed_grad = lax.dot_general(hidden_grad, up_weight, (((1,), (1,)), ((), ())), preferred_element_type=jnp.float32).reshape(conv.shape)
    gain_term = lax.optimization_barrier(jnp.sum(normed_grad * standard, axis=lead_axes))
    scaled_grad = normed_grad * norm_gain
    conv_grad = (inv_std * (scaled_grad - lax.optimization_barrier(jnp.mean(scaled_grad, axis=-1, keepdims=True)) - standard * lax.optimization_barrier(jnp.mean(scaled_grad * standard, axis=-1, keepdims=True)))).astype(jnp.bfloat16)
    kernel_term = kernel_sums(conv_grad, extended)
    grad_extended = extend_fn(conv_grad)
    input_grad = depthwise_transpose(grad_extended, conv_kernel)
    fields_grad = (upstream + maskf * input_grad).astype(jnp.bfloat16)
    return (block_out, fields_grad, (kernel_term, gain_term, up_term, bias_term, down_term, scale_term))

def reference(fields, cotangent, land_mask, neighbours, conv_kernel, norm_gain, up_weight, up_bias, down_weight, layer_scale):
    maskf = land_mask.astype(jnp.float32)[..., None]

    def extend_here(tile_data):
        return extend_tiles(tile_data, neighbours)

    def member(running_sum, inputs):
        field_member, cot_member = inputs
        masked = field_member * land_mask[..., None].astype(field_member.dtype)
        block_out, fields_grad, partials = block_pass(field_member, cot_member, maskf, extend_here(masked), extend_here, conv_kernel, norm_gain, up_weight, up_bias, down_weight, layer_scale)
        return (jax.tree.map(jnp.add, running_sum, partials), (block_out, fields_grad))
    channels = fields.shape[-1]
    hidden_units = up_weight.shape[1]
    zero_sums = (jnp.zeros((KERNEL, KERNEL, channels), jnp.float32), jnp.zeros((channels,), jnp.float32), jnp.zeros((channels, hidden_units), jnp.float32), jnp.zeros((hidden_units,), jnp.float32), jnp.zeros((hidden_units, channels), jnp.float32), jnp.zeros((channels,), jnp.float32))
    totals, (outputs, gradients) = lax.scan(member, zero_sums, (fields, cotangent))
    factor = 1.0 / math.sqrt(CELLS)
    return (outputs, gradients, totals[0] * factor, totals[1] * factor, totals[2] * factor, totals[3] * factor, totals[4] * factor, totals[5] * factor)
```

```python
import math

import jax
import jax.numpy as jnp
from jax import lax
from jax.sharding import PartitionSpec as P

KERNEL = 7
DILATION = 2
REACH = 3
HALO = 6


norm_eps = 1e-06
inv_sqrt_two = 0.7071067811865476
inv_sqrt_two_pi = 0.3989422804014327


def shifted(value, axis, steps):
    count = lax.axis_size(axis)
    leading, last = (max(0, -steps), min(count, count - steps))
    return lax.ppermute(value, axis, [(source, source + steps) for source in range(leading, last)])


def extend_tiles(centre, beside_ids, position):
    lead, rows, cols, channels = centre.shape
    top = centre[:, :HALO].reshape(lead, HALO * cols, channels)
    bottom = centre[:, -HALO:].reshape(lead, HALO * cols, channels)
    left = centre[:, :, :HALO].reshape(lead, rows * HALO, channels)
    right = centre[:, :, -HALO:].reshape(lead, rows * HALO, channels)
    west_step = beside_ids[2] - position
    east_step = beside_ids[3] - position
    has_west = beside_ids[2] >= 0
    has_east = beside_ids[3] >= 0
    received = []
    for step in (-3, -2, -1, 1, 2, 3):
        outgoing = top if step < 0 else bottom
        if abs(step) == 1:
            outgoing = jnp.where(has_west & (west_step == step), left, outgoing)
            outgoing = jnp.where(has_east & (east_step == step), right, outgoing)
        received.append((step, shifted(outgoing, "space", step)))
    pool = {-step: value for step, value in received}

    def choose(direction, steps):
        source = beside_ids[direction]
        strip = jnp.zeros_like(top)
        for step in steps:
            strip = jnp.where((source >= 0) & (source - position == step), pool[step], strip)
        return strip

    def as_rows(strip):
        return strip.reshape(lead, HALO, cols, channels)

    def as_cols(strip):
        return strip.reshape(lead, rows, HALO, channels)

    below, above = (-1, -2, -3), (1, 2, 3)
    north = as_rows(choose(0, below))
    south = as_rows(choose(1, above))
    west = as_cols(choose(2, (-1, 1)))
    east = as_cols(choose(3, (-1, 1)))
    north_west = as_rows(choose(4, below))[:, :, -HALO:]
    north_east = as_rows(choose(5, below))[:, :, :HALO]
    south_west = as_rows(choose(6, above))[:, :, -HALO:]
    south_east = as_rows(choose(7, above))[:, :, :HALO]
    upper = jnp.concatenate([north_west, north, north_east], axis=2)
    middle = jnp.concatenate([west, centre, east], axis=2)
    lower = jnp.concatenate([south_west, south, south_east], axis=2)
    return jnp.concatenate([upper, middle, lower], axis=1)


def summed_everywhere(flat):
    rows, lanes = flat.shape
    dp, space = lax.axis_size("dp"), lax.axis_size("space")
    part = lax.all_to_all(flat.reshape(dp, rows // dp, lanes), "dp", 0, 0, tiled=True)
    part = jnp.sum(part, axis=0).reshape(space, -1)
    part = jnp.sum(lax.all_to_all(part, "space", 0, 0, tiled=True), axis=0)
    part = jnp.broadcast_to(part, (space,) + part.shape)
    part = lax.all_to_all(part, "space", 0, 0, tiled=True).reshape(rows // dp, lanes)
    part = jnp.broadcast_to(part, (dp,) + part.shape)
    return lax.all_to_all(part, "dp", 0, 0, tiled=True).reshape(rows, lanes)


def depthwise(extended, conv_kernel):
    tile_rows = extended.shape[-3] - 2 * HALO
    tile_cols = extended.shape[-2] - 2 * HALO
    running = jnp.zeros(
        extended.shape[:-3] + (tile_rows, tile_cols, extended.shape[-1]), jnp.float32
    )
    for tap_row in range(KERNEL):
        for tap_col in range(KERNEL):
            window = extended[
                ...,
                DILATION * tap_row : DILATION * tap_row + tile_rows,
                DILATION * tap_col : DILATION * tap_col + tile_cols,
                :,
            ]
            running = running + conv_kernel[tap_row, tap_col] * window.astype(jnp.float32)
    return running


def depthwise_transpose(grad_extended, conv_kernel):
    tile_rows = grad_extended.shape[-3] - 2 * HALO
    tile_cols = grad_extended.shape[-2] - 2 * HALO
    running = jnp.zeros(
        grad_extended.shape[:-3] + (tile_rows, tile_cols, grad_extended.shape[-1]), jnp.float32
    )
    for tap_row in range(KERNEL):
        for tap_col in range(KERNEL):
            row_start = 2 * HALO - DILATION * tap_row
            col_start = 2 * HALO - DILATION * tap_col
            window = grad_extended[
                ..., row_start : row_start + tile_rows, col_start : col_start + tile_cols, :
            ]
            running = running + conv_kernel[tap_row, tap_col] * window.astype(jnp.float32)
    return running


def kernel_sums(conv_grad, extended):
    tile_rows = conv_grad.shape[-3]
    tile_cols = conv_grad.shape[-2]
    upstream = conv_grad.astype(jnp.float32)
    lead_axes = tuple(range(conv_grad.ndim - 1))
    rows_out = []
    for tap_row in range(KERNEL):
        row_terms = []
        for tap_col in range(KERNEL):
            window = extended[
                ...,
                DILATION * tap_row : DILATION * tap_row + tile_rows,
                DILATION * tap_col : DILATION * tap_col + tile_cols,
                :,
            ]
            row_terms.append(jnp.sum(upstream * window.astype(jnp.float32), axis=lead_axes))
        rows_out.append(jnp.stack(row_terms))
    return jnp.stack(rows_out)


def block_pass(
    fields,
    cotangent,
    maskf,
    extended,
    extend_fn,
    conv_kernel,
    norm_gain,
    up_weight,
    up_bias,
    down_weight,
    layer_scale,
):
    channels = fields.shape[-1]
    lead_axes = tuple(range(fields.ndim - 1))
    conv = depthwise(extended, conv_kernel)
    chan_mean = jnp.mean(conv, axis=-1, keepdims=True)
    centered = conv - chan_mean
    inv_std = lax.rsqrt(jnp.mean(centered * centered, axis=-1, keepdims=True) + norm_eps)
    standard = centered * inv_std
    normed = (standard * norm_gain).astype(jnp.bfloat16).reshape(-1, channels)
    hidden = jnp.dot(normed, up_weight, preferred_element_type=jnp.float32) + up_bias
    active = jax.nn.gelu(hidden, approximate=False).astype(jnp.bfloat16)
    branch = jnp.dot(active, down_weight, preferred_element_type=jnp.float32).reshape(fields.shape)
    block_out = (fields.astype(jnp.float32) + maskf * layer_scale * branch).astype(jnp.bfloat16)
    upstream = cotangent.astype(jnp.float32)
    scale_term = jnp.sum(maskf * branch * upstream, axis=lead_axes)
    branch_grad = (maskf * layer_scale * upstream).astype(jnp.bfloat16).reshape(-1, channels)
    down_term = lax.dot_general(
        active, branch_grad, (((0,), (0,)), ((), ())), preferred_element_type=jnp.float32
    )
    active_grad = lax.dot_general(
        branch_grad, down_weight, (((1,), (1,)), ((), ())), preferred_element_type=jnp.float32
    )
    gelu_slope = (
        0.5 * (1.0 + lax.erf(hidden * inv_sqrt_two))
        + hidden * jnp.exp(-0.5 * hidden * hidden) * inv_sqrt_two_pi
    )
    hidden_grad = (active_grad * gelu_slope).astype(jnp.bfloat16)
    up_term = lax.dot_general(
        normed, hidden_grad, (((0,), (0,)), ((), ())), preferred_element_type=jnp.float32
    )
    bias_term = jnp.sum(hidden_grad.astype(jnp.float32), axis=0)
    normed_grad = lax.dot_general(
        hidden_grad, up_weight, (((1,), (1,)), ((), ())), preferred_element_type=jnp.float32
    ).reshape(conv.shape)
    gain_term = jnp.sum(normed_grad * standard, axis=lead_axes)
    scaled_grad = normed_grad * norm_gain
    conv_grad = (
        inv_std
        * (
            scaled_grad
            - jnp.mean(scaled_grad, axis=-1, keepdims=True)
            - standard * jnp.mean(scaled_grad * standard, axis=-1, keepdims=True)
        )
    ).astype(jnp.bfloat16)
    kernel_term = kernel_sums(conv_grad, extended)
    grad_extended = extend_fn(conv_grad)
    input_grad = depthwise_transpose(grad_extended, conv_kernel)
    fields_grad = (upstream + maskf * input_grad).astype(jnp.bfloat16)
    return (
        block_out,
        fields_grad,
        (kernel_term, gain_term, up_term, bias_term, down_term, scale_term),
    )


def local(
    fields,
    cotangent,
    land_mask,
    neighbours,
    conv_kernel,
    norm_gain,
    up_weight,
    up_bias,
    down_weight,
    layer_scale,
):
    position = lax.axis_index("space")
    beside_ids = neighbours[0]
    maskf = land_mask.astype(jnp.float32)[..., None]
    centre = fields[:, 0]
    masked = centre * land_mask.astype(jnp.bfloat16)[..., None]

    def extend_here(tile_data):
        return extend_tiles(tile_data, beside_ids, position)

    block_out, fields_grad, partials = block_pass(
        centre,
        cotangent[:, 0],
        maskf,
        extend_here(masked),
        extend_here,
        conv_kernel,
        norm_gain,
        up_weight,
        up_bias,
        down_weight,
        layer_scale,
    )
    leaves = [leaf.reshape(-1, 128) for leaf in partials]
    counts = [leaf.shape[0] for leaf in leaves]
    unit = lax.axis_size("dp") * 4
    spare = -sum(counts) % unit
    flat = jnp.concatenate(leaves + [jnp.zeros((spare, 128), jnp.float32)], axis=0)
    flat = summed_everywhere(flat)
    totals, at = [], 0
    for leaf, count in zip(partials, counts):
        totals.append(flat[at : at + count].reshape(leaf.shape))
        at += count
    cell_count = (
        fields.shape[0]
        * lax.axis_size("dp")
        * lax.axis_size("space")
        * fields.shape[2]
        * fields.shape[3]
    )
    factor = 1.0 / math.sqrt(cell_count)
    return (
        block_out[:, None],
        fields_grad[:, None],
        totals[0] * factor,
        totals[1] * factor,
        totals[2] * factor,
        totals[3] * factor,
        totals[4] * factor,
        totals[5] * factor,
    )


def solution(mesh):
    return jax.shard_map(
        local,
        mesh=mesh,
        in_specs=(
            P("dp", "space", None, None, None),
            P("dp", "space", None, None, None),
            P("space", None, None),
            P("space", None),
            P(),
            P(),
            P(),
            P(),
            P(),
            P(),
        ),
        out_specs=(
            P("dp", "space", None, None, None),
            P("dp", "space", None, None, None),
            P(),
            P(),
            P(),
            P(),
            P(),
            P(),
        ),
        check_vma=False,
    )
```

```python
import math

import jax
import jax.numpy as jnp
from jax import lax
from jax.experimental import pallas as pl
from jax.experimental.pallas import tpu as pltpu
from jax.sharding import PartitionSpec as P

KERNEL = 7
DILATION = 2
HALO = 6
TAPS = KERNEL * KERNEL
TILE = 48
LANES = 128
PAD = 2
EXT_ROWS = TILE + 2 * HALO
EXT_COLS = 64
CHUNK = 8
CELLS_IN_CHUNK = CHUNK * TILE
GROUPS = TILE // 8
STEPS = (-3, -2, -1, 1, 2, 3)

norm_eps = 1e-06
inv_sqrt_two_pi = 0.3989422804014327
TAIL_RATE = 0.3889087296526013
TAIL_TERMS = (
    0.15079174476614957,
    0.19542085643011212,
    -0.02071252121020706,
    0.379856419408137,
    -0.25901857729927547,
    0.05366208632016299,
)

f32 = jnp.float32
bf16 = jnp.bfloat16
VMEM = pl.BlockSpec(memory_space=pltpu.VMEM)
SMEM = pl.BlockSpec(memory_space=pltpu.SMEM)


def pack_strips(flat, beside, where, top, bottom, to_before, to_after):
    position = where[0]
    upper = flat[0 : HALO * TILE, :].astype(bf16).reshape(HALO, TILE, LANES)
    lower = flat[(TILE - HALO) * TILE :, :].astype(bf16).reshape(HALO, TILE, LANES)
    top[...] = upper
    bottom[...] = lower
    to_before[...] = upper
    to_after[...] = lower

    def columns(out, first):
        for c in range(HALO):
            parts = [
                flat[pl.ds(8 * g * TILE + first + c, 8, stride=TILE), :] for g in range(GROUPS)
            ]
            out[c] = jnp.concatenate(parts, axis=0).astype(bf16)

    for out, step in ((to_before, -1), (to_after, 1)):
        for direction, first in ((2, 0), (3, TILE - HALO)):
            source = beside[direction]

            @pl.when((source >= 0) & (source - position == step))
            def _(out=out, first=first):
                columns(out, first)


def place_rims(ext, ext_flat, beside, where, strips):
    position = where[0]
    zero_rows = jnp.zeros((HALO, EXT_COLS, LANES), f32)
    zero_cols = jnp.zeros((TILE, 8, LANES), f32)
    ext[0:HALO] = zero_rows
    ext[HALO + TILE :] = zero_rows
    ext[HALO : HALO + TILE, 0:8, :] = zero_cols
    ext[HALO : HALO + TILE, 8 + TILE :, :] = zero_cols
    last = TILE - 8

    def put_rows(first):
        def put(strip):
            ext[first : first + HALO, 8 : 8 + TILE, :] = strip.astype(f32)

        return put

    def put_corner(first, east):
        def put(strip):
            wide = strip.astype(f32)
            if east:
                ext[first : first + HALO, 8 + TILE :, :] = wide[:, 0:8]
            else:
                ext[first : first + HALO, 0:8, :] = wide[:, last:]

        return put

    def put_columns(first):
        def put(strip):
            wide = strip.astype(f32)
            for c in range(HALO):
                for g in range(GROUPS):
                    at = (HALO + 8 * g) * EXT_COLS + first + c
                    ext_flat[pl.ds(at, 8, stride=EXT_COLS), :] = wide[c, 8 * g : 8 * g + 8]

        return put

    south_row = HALO + TILE
    before, after = (-1, -2, -3), (1, 2, 3)
    for direction, steps, put in (
        (4, before, put_corner(0, False)),
        (5, before, put_corner(0, True)),
        (6, after, put_corner(south_row, False)),
        (7, after, put_corner(south_row, True)),
        (0, before, put_rows(0)),
        (1, after, put_rows(south_row)),
        (2, (-1, 1), put_columns(PAD)),
        (3, (-1, 1), put_columns(8 + TILE)),
    ):
        source = beside[direction]
        for step in steps:

            @pl.when((source >= 0) & (source - position == step))
            def _(step=step, put=put):
                put(strips[STEPS.index(step)][...])


def conv_group(ext, weights, first_row, g):
    sums = [None] * CHUNK
    for b in range(KERNEL):
        taps = [
            jnp.broadcast_to(weights[a * KERNEL + b : a * KERNEL + b + 1, :], (8, LANES))
            for a in range(KERNEL)
        ]
        column = PAD + 8 * g + DILATION * b
        for i in range(CHUNK + 2 * HALO):
            window = ext[first_row + i, pl.ds(column, 8), :]
            for a in range(KERNEL):
                row = i - DILATION * a
                if 0 <= row < CHUNK:
                    term = taps[a] * window
                    sums[row] = term if sums[row] is None else sums[row] + term
    return sums


def pack_kernel(beside, where, fields, mask, top, bottom, to_before, to_after, flat):
    def rows(i, _):
        cells = pl.ds(pl.multiple_of(i * TILE, TILE), TILE)
        flat[cells, :] = fields[i].astype(f32) * mask[i].astype(f32)
        return 0

    lax.fori_loop(0, TILE, rows, 0, unroll=4)
    pack_strips(flat, beside, where, top, bottom, to_before, to_after)


def block_kernel(
    beside,
    where,
    fields,
    cotangent,
    mask,
    s0,
    s1,
    s2,
    s3,
    s4,
    s5,
    weights,
    gain,
    up_weight,
    up_bias,
    down_weight,
    scale,
    block_out,
    conv_grad,
    top,
    bottom,
    to_before,
    to_after,
    sums,
    ext,
    grad_flat,
    standard,
    inv_std,
    normed,
    branch_grad,
    hidden,
    active_grad,
    active,
    hidden_grad,
    up_sum,
    down_sum,
    bias_sum,
    tap_sums,
    row_sums,
):
    ext_flat = ext.reshape(EXT_ROWS * EXT_COLS, LANES)

    def centre(i, _):
        ext[HALO + i, pl.ds(8, TILE), :] = fields[i].astype(f32) * mask[i].astype(f32)
        return 0

    lax.fori_loop(0, TILE, centre, 0, unroll=4)
    place_rims(ext, ext_flat, beside, where, (s0, s1, s2, s3, s4, s5))
    up_sum[...] = jnp.zeros_like(up_sum)
    down_sum[...] = jnp.zeros_like(down_sum)
    bias_sum[...] = jnp.zeros_like(bias_sum)
    tap_sums[...] = jnp.zeros_like(tap_sums)
    row_sums[...] = jnp.zeros_like(row_sums)
    ones = jnp.ones((8, CELLS_IN_CHUNK), bf16)

    def chunk(step, _):
        first = pl.multiple_of(step * CHUNK, CHUNK)
        for g in range(GROUPS):
            values = conv_group(ext, weights, first, g)
            for row in range(CHUNK):
                standard[pl.ds(row * TILE + 8 * g, 8), :] = values[row]

        def normalise(row, _):
            cells = pl.ds(pl.multiple_of(row * TILE, TILE), TILE)
            conv = standard[cells, :]
            centered = conv - jnp.mean(conv, axis=-1, keepdims=True)
            inv = lax.rsqrt(jnp.mean(centered * centered, axis=-1, keepdims=True) + norm_eps)
            unit = centered * inv
            standard[cells, :] = unit
            inv_std[cells, :] = jnp.broadcast_to(inv, (TILE, LANES))
            normed[cells, :] = (unit * gain[...]).astype(bf16)
            weighted = mask[first + row].astype(f32) * scale[...]
            branch_grad[cells, :] = (weighted * cotangent[first + row].astype(f32)).astype(bf16)
            return 0

        lax.fori_loop(0, CHUNK, normalise, 0, unroll=2)
        hidden[...] = jnp.dot(normed[...], up_weight[...], preferred_element_type=f32)
        active_grad[...] = lax.dot_general(
            branch_grad[...],
            down_weight[...],
            (((1,), (1,)), ((), ())),
            preferred_element_type=f32,
        )

        def activate(i, _):
            cells = pl.ds(pl.multiple_of(i * 16, 16), 16)
            h = hidden[cells, :] + up_bias[...]
            t = pl.reciprocal(1.0 + TAIL_RATE * jnp.abs(h), approx=False)
            tail = TAIL_TERMS[-1] * t + TAIL_TERMS[-2]
            for term in TAIL_TERMS[-3::-1]:
                tail = tail * t + term
            bell = jnp.exp(-0.5 * h * h)
            tail = tail * t * bell
            phi = jnp.where(h >= 0, 1.0 - tail, tail)
            active[cells, :] = (h * phi).astype(bf16)
            slope = phi + h * (bell * inv_sqrt_two_pi)
            hidden_grad[cells, :] = (active_grad[cells, :] * slope).astype(bf16)
            return 0

        lax.fori_loop(0, CELLS_IN_CHUNK // 16, activate, 0, unroll=2)
        hidden[:, 0:LANES] = jnp.dot(active[...], down_weight[...], preferred_element_type=f32)
        active_grad[:, 0:LANES] = lax.dot_general(
            hidden_grad[...], up_weight[...], (((1,), (1,)), ((), ())), preferred_element_type=f32
        )
        over_cells = (((0,), (0,)), ((), ()))
        down_sum[...] += lax.dot_general(
            branch_grad[...], active[...], over_cells, preferred_element_type=f32
        )
        up_sum[...] += lax.dot_general(
            normed[...], hidden_grad[...], over_cells, preferred_element_type=f32
        )
        bias_sum[...] += jnp.dot(ones, hidden_grad[...], preferred_element_type=f32)

        def finish(row, _):
            cells = pl.ds(pl.multiple_of(row * TILE, TILE), TILE)
            at = first + row
            masked_branch = mask[at].astype(f32) * hidden[cells, 0:LANES]
            block_out[at] = (fields[at].astype(f32) + masked_branch * scale[...]).astype(bf16)
            by_scale = masked_branch * cotangent[at].astype(f32)
            unit = standard[cells, :]
            grad = active_grad[cells, 0:LANES]
            by_gain = grad * unit
            u = grad * gain[...]
            mean_u = jnp.mean(u, axis=-1, keepdims=True)
            mean_us = jnp.mean(u * unit, axis=-1, keepdims=True)
            out = (inv_std[cells, :] * (u - mean_u - unit * mean_us)).astype(bf16)
            conv_grad[at] = out
            grad_flat[pl.ds(pl.multiple_of(at * TILE, TILE), TILE), :] = out.astype(f32)
            for k in range(GROUPS):
                row_sums[0:8, :] += by_scale[8 * k : 8 * k + 8]
                row_sums[8:16, :] += by_gain[8 * k : 8 * k + 8]
            return 0

        lax.fori_loop(0, CHUNK, finish, 0, unroll=2)
        for b in range(KERNEL):
            totals = [tap_sums[a * KERNEL + b] for a in range(KERNEL)]
            for g in range(GROUPS):
                grads = [
                    grad_flat[pl.ds((first + row) * TILE + 8 * g, 8), :] for row in range(CHUNK)
                ]
                column = PAD + 8 * g + DILATION * b
                for i in range(CHUNK + 2 * HALO):
                    window = ext[first + i, pl.ds(column, 8), :]
                    for a in range(KERNEL):
                        row = i - DILATION * a
                        if 0 <= row < CHUNK:
                            totals[a] = totals[a] + grads[row] * window
            for a in range(KERNEL):
                tap_sums[a * KERNEL + b] = totals[a]
        return 0

    lax.fori_loop(0, TILE // CHUNK, chunk, 0)
    pack_strips(grad_flat, beside, where, top, bottom, to_before, to_after)

    quarters = up_sum.shape[1] // LANES
    for q in range(quarters):
        lanes = slice(q * LANES, (q + 1) * LANES)
        sums[q * LANES : (q + 1) * LANES, :] = up_sum[:, lanes]
        sums[(quarters + q) * LANES : (quarters + q + 1) * LANES, :] = down_sum[:, lanes]
    at = 2 * quarters * LANES
    sums[at:, :] = jnp.zeros((sums.shape[0] - at, LANES), f32)
    sums[at : at + TAPS, :] = jnp.sum(tap_sums[...], axis=1)
    sums[at + TAPS : at + TAPS + 1, :] = jnp.sum(row_sums[0:8, :], axis=0, keepdims=True)
    sums[at + TAPS + 1 : at + TAPS + 2, :] = jnp.sum(row_sums[8:16, :], axis=0, keepdims=True)
    for q in range(quarters):
        row = at + TAPS + 2 + q
        sums[row : row + 1, :] = bias_sum[0:1, q * LANES : (q + 1) * LANES]


def back_kernel(
    beside, where, conv_grad, cotangent, mask, s0, s1, s2, s3, s4, s5, weights, fields_grad, ext
):
    ext_flat = ext.reshape(EXT_ROWS * EXT_COLS, LANES)

    def centre(i, _):
        ext[HALO + i, pl.ds(8, TILE), :] = conv_grad[i].astype(f32)
        return 0

    lax.fori_loop(0, TILE, centre, 0, unroll=4)
    place_rims(ext, ext_flat, beside, where, (s0, s1, s2, s3, s4, s5))

    def chunk(step, _):
        first = pl.multiple_of(step * CHUNK, CHUNK)
        columns = [conv_group(ext, weights, first, g) for g in range(GROUPS)]
        for row in range(CHUNK):
            at = first + row
            whole = jnp.concatenate([columns[g][row] for g in range(GROUPS)], axis=0)
            out = cotangent[at].astype(f32) + mask[at].astype(f32) * whole
            fields_grad[at] = out.astype(bf16)
        return 0

    lax.fori_loop(0, TILE // CHUNK, chunk, 0)


def shape(dims, dtype=bf16):
    return jax.ShapeDtypeStruct(dims, dtype)


STRIP = (HALO, TILE, LANES)
WHOLE = (TILE, TILE, LANES)


def call(kernel, scalars, operands, outs, scratch, flops, limit):
    size = sum(math.prod(a.shape) * a.dtype.itemsize for a in (*operands, *outs))
    return pl.pallas_call(
        kernel,
        out_shape=outs,
        in_specs=[SMEM] * len(scalars) + [VMEM] * len(operands),
        out_specs=[VMEM] * len(outs),
        scratch_shapes=scratch,
        compiler_params=pltpu.CompilerParams(vmem_limit_bytes=limit * 2**20),
        cost_estimate=pl.CostEstimate(flops=flops, bytes_accessed=size, transcendentals=0),
    )(*scalars, *operands)


def shifted(value, step):
    count = lax.axis_size("space")
    first, last = (max(0, -step), min(count, count - step))
    return lax.ppermute(value, "space", [(source, source + step) for source in range(first, last)])


def exchange(top, bottom, to_before, to_after):
    sent = {3: bottom, 2: bottom, 1: to_after, -1: to_before, -2: top, -3: top}
    return [shifted(sent[-step], -step) for step in STEPS]


def summed_everywhere(flat, factor):
    rows, lanes = flat.shape
    dp, space = lax.axis_size("dp"), lax.axis_size("space")
    part = lax.all_to_all(flat.reshape(dp, rows // dp, lanes), "dp", 0, 0, tiled=True)
    part = jnp.sum(part, axis=0).reshape(space, -1)
    part = jnp.sum(lax.all_to_all(part, "space", 0, 0, tiled=True), axis=0) * factor
    part = jnp.broadcast_to(part, (space,) + part.shape)
    part = lax.all_to_all(part, "space", 0, 0, tiled=True).reshape(rows // dp, lanes)
    part = jnp.broadcast_to(part, (dp,) + part.shape)
    return lax.all_to_all(part, "dp", 0, 0, tiled=True).reshape(rows, lanes)


def local(
    fields,
    cotangent,
    land_mask,
    neighbours,
    conv_kernel,
    norm_gain,
    up_weight,
    up_bias,
    down_weight,
    layer_scale,
):
    beside = neighbours[0]
    where = lax.axis_index("space").astype(jnp.int32)[None]
    tile, upstream = fields[0, 0], cotangent[0, 0]
    mask = jnp.broadcast_to(land_mask[0].astype(bf16)[..., None], WHOLE)
    taps = conv_kernel.reshape(TAPS, LANES)
    units = up_weight.shape[1]
    quarters = units // LANES
    sum_rows = -(-(2 * units + TAPS + 2 + quarters) // 64) * 64

    rims = call(
        pack_kernel,
        (beside, where),
        (tile, mask),
        [shape(STRIP)] * 4,
        [pltpu.VMEM((TILE * TILE, LANES), f32)],
        TILE * TILE * LANES,
        32,
    )
    strips = exchange(*rims)
    block_out, conv_grad, *rims, sums = call(
        block_kernel,
        (beside, where),
        (
            tile,
            upstream,
            mask,
            *strips,
            taps,
            norm_gain[None],
            up_weight,
            up_bias[None],
            down_weight,
            layer_scale[None],
        ),
        [shape(WHOLE), shape(WHOLE)] + [shape(STRIP)] * 4 + [shape((sum_rows, LANES), f32)],
        [
            pltpu.VMEM((EXT_ROWS, EXT_COLS, LANES), f32),
            pltpu.VMEM((TILE * TILE, LANES), f32),
            pltpu.VMEM((CELLS_IN_CHUNK, LANES), f32),
            pltpu.VMEM((CELLS_IN_CHUNK, LANES), f32),
            pltpu.VMEM((CELLS_IN_CHUNK, LANES), bf16),
            pltpu.VMEM((CELLS_IN_CHUNK, LANES), bf16),
            pltpu.VMEM((CELLS_IN_CHUNK, units), f32),
            pltpu.VMEM((CELLS_IN_CHUNK, units), f32),
            pltpu.VMEM((CELLS_IN_CHUNK, units), bf16),
            pltpu.VMEM((CELLS_IN_CHUNK, units), bf16),
            pltpu.VMEM((LANES, units), f32),
            pltpu.VMEM((LANES, units), f32),
            pltpu.VMEM((8, units), f32),
            pltpu.VMEM((TAPS, 8, LANES), f32),
            pltpu.VMEM((16, LANES), f32),
        ],
        12 * TILE * TILE * LANES * units,
        40,
    )
    strips = exchange(*rims)
    cells = TILE * TILE * lax.axis_size("dp") * lax.axis_size("space")
    total = summed_everywhere(sums, 1.0 / math.sqrt(cells))
    (fields_grad,) = call(
        back_kernel,
        (beside, where),
        (conv_grad, upstream, mask, *strips, taps[::-1]),
        [shape(WHOLE)],
        [pltpu.VMEM((EXT_ROWS, EXT_COLS, LANES), f32)],
        2 * TAPS * TILE * TILE * LANES,
        32,
    )
    up_grad = total[:units].reshape(quarters, LANES, LANES).transpose(1, 0, 2).reshape(LANES, units)
    down_grad = total[units : 2 * units].reshape(quarters, LANES, LANES).transpose(0, 2, 1)
    at = 2 * units
    return (
        block_out[None, None],
        fields_grad[None, None],
        total[at : at + TAPS].reshape(KERNEL, KERNEL, LANES),
        total[at + TAPS + 1],
        up_grad,
        total[at + TAPS + 2 : at + TAPS + 2 + quarters].reshape(units),
        down_grad.reshape(units, LANES),
        total[at + TAPS],
    )


def solution(mesh):
    tiles = P("dp", "space", None, None, None)
    return jax.shard_map(
        local,
        mesh=mesh,
        in_specs=(
            tiles,
            tiles,
            P("space", None, None),
            P("space", None),
            P(),
            P(),
            P(),
            P(),
            P(),
            P(),
        ),
        out_specs=(tiles, tiles, P(), P(), P(), P(), P(), P()),
        check_vma=False,
    )
```

```python
import math

import jax
import jax.numpy as jnp
from jax import lax
from jax.experimental import pallas as pl
from jax.experimental.pallas import tpu as pltpu
from jax.sharding import PartitionSpec as P

KERNEL = 7
DILATION = 2
HALO = 6
TAPS = KERNEL * KERNEL
TILE = 48
LANES = 128
PAD = 2
EXT_ROWS = TILE + 2 * HALO
EXT_COLS = 64
CHUNK = 8
CELLS_IN_CHUNK = CHUNK * TILE
GROUPS = TILE // 8
STEPS = (-3, -2, -1, 1, 2, 3)
VMEM_LIMIT = 32 * 2**20
DP = ("x_hi", "y", "core")
SPACE = ("z", "x_lo")
PLANE = ("x_hi", "y", "core", "x_lo")

norm_eps = 1e-06
inv_sqrt_two_pi = 0.3989422804014327
TAIL_RATE = 0.3889087296526013
TAIL_TERMS = (
    0.15079174476614957,
    0.19542085643011212,
    -0.02071252121020706,
    0.379856419408137,
    -0.25901857729927547,
    0.05366208632016299,
)

f32 = jnp.float32
bf16 = jnp.bfloat16
VMEM = pl.BlockSpec(memory_space=pltpu.VMEM)
SMEM = pl.BlockSpec(memory_space=pltpu.SMEM)


def pack_strips(flat, beside, where, top, bottom, to_before, to_after):
    position = where[0]
    upper = flat[0 : HALO * TILE, :].astype(bf16).reshape(HALO, TILE, LANES)
    lower = flat[(TILE - HALO) * TILE :, :].astype(bf16).reshape(HALO, TILE, LANES)
    top[...] = upper
    bottom[...] = lower
    to_before[...] = upper
    to_after[...] = lower

    def columns(out, first):
        for c in range(HALO):
            parts = [
                flat[pl.ds(8 * g * TILE + first + c, 8, stride=TILE), :] for g in range(GROUPS)
            ]
            out[c] = jnp.concatenate(parts, axis=0).astype(bf16)

    for out, step in ((to_before, -1), (to_after, 1)):
        for direction, first in ((2, 0), (3, TILE - HALO)):
            source = beside[direction]

            @pl.when((source >= 0) & (source - position == step))
            def _(out=out, first=first):
                columns(out, first)


def place_rims(ext, ext_flat, beside, where, strips):
    position = where[0]
    zero_rows = jnp.zeros((HALO, EXT_COLS, LANES), f32)
    zero_cols = jnp.zeros((TILE, 8, LANES), f32)
    ext[0:HALO] = zero_rows
    ext[HALO + TILE :] = zero_rows
    ext[HALO : HALO + TILE, 0:8, :] = zero_cols
    ext[HALO : HALO + TILE, 8 + TILE :, :] = zero_cols
    last = TILE - 8

    def put_rows(first):
        def put(strip):
            ext[first : first + HALO, 8 : 8 + TILE, :] = strip.astype(f32)

        return put

    def put_corner(first, east):
        def put(strip):
            wide = strip.astype(f32)
            if east:
                ext[first : first + HALO, 8 + TILE :, :] = wide[:, 0:8]
            else:
                ext[first : first + HALO, 0:8, :] = wide[:, last:]

        return put

    def put_columns(first):
        def put(strip):
            wide = strip.astype(f32)
            for c in range(HALO):
                for g in range(GROUPS):
                    at = (HALO + 8 * g) * EXT_COLS + first + c
                    ext_flat[pl.ds(at, 8, stride=EXT_COLS), :] = wide[c, 8 * g : 8 * g + 8]

        return put

    south_row = HALO + TILE
    before, after = (-1, -2, -3), (1, 2, 3)
    for direction, steps, put in (
        (4, before, put_corner(0, False)),
        (5, before, put_corner(0, True)),
        (6, after, put_corner(south_row, False)),
        (7, after, put_corner(south_row, True)),
        (0, before, put_rows(0)),
        (1, after, put_rows(south_row)),
        (2, (-1, 1), put_columns(PAD)),
        (3, (-1, 1), put_columns(8 + TILE)),
    ):
        source = beside[direction]
        for step in steps:

            @pl.when((source >= 0) & (source - position == step))
            def _(step=step, put=put):
                put(strips[STEPS.index(step)][...])


def conv_group(ext, weights, first_row, g):
    sums = [None] * CHUNK
    for b in range(KERNEL):
        taps = [
            jnp.broadcast_to(weights[a * KERNEL + b : a * KERNEL + b + 1, :], (8, LANES))
            for a in range(KERNEL)
        ]
        column = PAD + 8 * g + DILATION * b
        for i in range(CHUNK + 2 * HALO):
            window = ext[first_row + i, pl.ds(column, 8), :]
            for a in range(KERNEL):
                row = i - DILATION * a
                if 0 <= row < CHUNK:
                    term = taps[a] * window
                    sums[row] = term if sums[row] is None else sums[row] + term
    return sums


def pack_kernel(beside, where, fields, mask, top, bottom, to_before, to_after, flat):
    def rows(i, _):
        cells = pl.ds(pl.multiple_of(i * TILE, TILE), TILE)
        flat[cells, :] = fields[i].astype(f32) * mask[i].astype(f32)
        return 0

    lax.fori_loop(0, TILE, rows, 0, unroll=4)
    pack_strips(flat, beside, where, top, bottom, to_before, to_after)


def block_kernel(
    beside,
    where,
    fields,
    cotangent,
    mask,
    s0,
    s1,
    s2,
    s3,
    s4,
    s5,
    weights,
    gain,
    up_weight,
    up_bias,
    down_weight,
    scale,
    block_out,
    conv_grad,
    top,
    bottom,
    to_before,
    to_after,
    sums,
    ext,
    grad_flat,
    standard,
    inv_std,
    normed,
    branch_grad,
    hidden,
    active_grad,
    active,
    hidden_grad,
    up_sum,
    down_sum,
    bias_sum,
    tap_sums,
    row_sums,
):
    ext_flat = ext.reshape(EXT_ROWS * EXT_COLS, LANES)

    def centre(i, _):
        ext[HALO + i, pl.ds(8, TILE), :] = fields[i].astype(f32) * mask[i].astype(f32)
        return 0

    lax.fori_loop(0, TILE, centre, 0, unroll=4)
    place_rims(ext, ext_flat, beside, where, (s0, s1, s2, s3, s4, s5))
    up_sum[...] = jnp.zeros_like(up_sum)
    down_sum[...] = jnp.zeros_like(down_sum)
    bias_sum[...] = jnp.zeros_like(bias_sum)
    tap_sums[...] = jnp.zeros_like(tap_sums)
    row_sums[...] = jnp.zeros_like(row_sums)
    ones = jnp.ones((8, CELLS_IN_CHUNK), bf16)

    def chunk(step, _):
        first = pl.multiple_of(step * CHUNK, CHUNK)
        for g in range(GROUPS):
            values = conv_group(ext, weights, first, g)
            for row in range(CHUNK):
                standard[pl.ds(row * TILE + 8 * g, 8), :] = values[row]

        def normalise(row, _):
            cells = pl.ds(pl.multiple_of(row * TILE, TILE), TILE)
            conv = standard[cells, :]
            centered = conv - jnp.mean(conv, axis=-1, keepdims=True)
            inv = lax.rsqrt(jnp.mean(centered * centered, axis=-1, keepdims=True) + norm_eps)
            unit = centered * inv
            standard[cells, :] = unit
            inv_std[cells, :] = jnp.broadcast_to(inv, (TILE, LANES))
            normed[cells, :] = (unit * gain[...]).astype(bf16)
            weighted = mask[first + row].astype(f32) * scale[...]
            branch_grad[cells, :] = (weighted * cotangent[first + row].astype(f32)).astype(bf16)
            return 0

        lax.fori_loop(0, CHUNK, normalise, 0, unroll=2)
        hidden[...] = jnp.dot(normed[...], up_weight[...], preferred_element_type=f32)
        active_grad[...] = lax.dot_general(
            branch_grad[...],
            down_weight[...],
            (((1,), (1,)), ((), ())),
            preferred_element_type=f32,
        )

        def activate(i, _):
            cells = pl.ds(pl.multiple_of(i * 16, 16), 16)
            h = hidden[cells, :] + up_bias[...]
            t = pl.reciprocal(1.0 + TAIL_RATE * jnp.abs(h), approx=False)
            tail = TAIL_TERMS[-1] * t + TAIL_TERMS[-2]
            for term in TAIL_TERMS[-3::-1]:
                tail = tail * t + term
            bell = jnp.exp(-0.5 * h * h)
            tail = tail * t * bell
            phi = jnp.where(h >= 0, 1.0 - tail, tail)
            active[cells, :] = (h * phi).astype(bf16)
            slope = phi + h * (bell * inv_sqrt_two_pi)
            hidden_grad[cells, :] = (active_grad[cells, :] * slope).astype(bf16)
            return 0

        lax.fori_loop(0, CELLS_IN_CHUNK // 16, activate, 0, unroll=2)
        hidden[:, 0:LANES] = jnp.dot(active[...], down_weight[...], preferred_element_type=f32)
        active_grad[:, 0:LANES] = lax.dot_general(
            hidden_grad[...], up_weight[...], (((1,), (1,)), ((), ())), preferred_element_type=f32
        )
        over_cells = (((0,), (0,)), ((), ()))
        down_sum[...] += lax.dot_general(
            branch_grad[...], active[...], over_cells, preferred_element_type=f32
        )
        up_sum[...] += lax.dot_general(
            normed[...], hidden_grad[...], over_cells, preferred_element_type=f32
        )
        bias_sum[...] += jnp.dot(ones, hidden_grad[...], preferred_element_type=f32)

        def finish(row, _):
            cells = pl.ds(pl.multiple_of(row * TILE, TILE), TILE)
            at = first + row
            masked_branch = mask[at].astype(f32) * hidden[cells, 0:LANES]
            block_out[at] = (fields[at].astype(f32) + masked_branch * scale[...]).astype(bf16)
            by_scale = masked_branch * cotangent[at].astype(f32)
            unit = standard[cells, :]
            grad = active_grad[cells, 0:LANES]
            by_gain = grad * unit
            u = grad * gain[...]
            mean_u = jnp.mean(u, axis=-1, keepdims=True)
            mean_us = jnp.mean(u * unit, axis=-1, keepdims=True)
            out = (inv_std[cells, :] * (u - mean_u - unit * mean_us)).astype(bf16)
            conv_grad[at] = out
            grad_flat[pl.ds(pl.multiple_of(at * TILE, TILE), TILE), :] = out.astype(f32)
            for k in range(GROUPS):
                row_sums[0:8, :] += by_scale[8 * k : 8 * k + 8]
                row_sums[8:16, :] += by_gain[8 * k : 8 * k + 8]
            return 0

        lax.fori_loop(0, CHUNK, finish, 0, unroll=2)
        for b in range(KERNEL):
            totals = [tap_sums[a * KERNEL + b] for a in range(KERNEL)]
            for g in range(GROUPS):
                grads = [
                    grad_flat[pl.ds((first + row) * TILE + 8 * g, 8), :] for row in range(CHUNK)
                ]
                column = PAD + 8 * g + DILATION * b
                for i in range(CHUNK + 2 * HALO):
                    window = ext[first + i, pl.ds(column, 8), :]
                    for a in range(KERNEL):
                        row = i - DILATION * a
                        if 0 <= row < CHUNK:
                            totals[a] = totals[a] + grads[row] * window
            for a in range(KERNEL):
                tap_sums[a * KERNEL + b] = totals[a]
        return 0

    lax.fori_loop(0, TILE // CHUNK, chunk, 0)
    pack_strips(grad_flat, beside, where, top, bottom, to_before, to_after)

    quarters = up_sum.shape[1] // LANES
    for q in range(quarters):
        lanes = slice(q * LANES, (q + 1) * LANES)
        sums[q * LANES : (q + 1) * LANES, :] = up_sum[:, lanes]
        sums[(quarters + q) * LANES : (quarters + q + 1) * LANES, :] = down_sum[:, lanes].T
    at = 2 * quarters * LANES
    sums[at:, :] = jnp.zeros((sums.shape[0] - at, LANES), f32)
    sums[at : at + TAPS, :] = jnp.sum(tap_sums[...], axis=1)
    sums[at + TAPS : at + TAPS + 1, :] = jnp.sum(row_sums[0:8, :], axis=0, keepdims=True)
    sums[at + TAPS + 1 : at + TAPS + 2, :] = jnp.sum(row_sums[8:16, :], axis=0, keepdims=True)
    for q in range(quarters):
        row = at + TAPS + 2 + q
        sums[row : row + 1, :] = bias_sum[0:1, q * LANES : (q + 1) * LANES]


def back_kernel(
    beside, where, conv_grad, cotangent, mask, s0, s1, s2, s3, s4, s5, weights, fields_grad, ext
):
    ext_flat = ext.reshape(EXT_ROWS * EXT_COLS, LANES)

    def centre(i, _):
        ext[HALO + i, pl.ds(8, TILE), :] = conv_grad[i].astype(f32)
        return 0

    lax.fori_loop(0, TILE, centre, 0, unroll=4)
    place_rims(ext, ext_flat, beside, where, (s0, s1, s2, s3, s4, s5))

    def chunk(step, _):
        first = pl.multiple_of(step * CHUNK, CHUNK)
        columns = [conv_group(ext, weights, first, g) for g in range(GROUPS)]
        for row in range(CHUNK):
            at = first + row
            whole = jnp.concatenate([columns[g][row] for g in range(GROUPS)], axis=0)
            out = cotangent[at].astype(f32) + mask[at].astype(f32) * whole
            fields_grad[at] = out.astype(bf16)
        return 0

    lax.fori_loop(0, TILE // CHUNK, chunk, 0)


def unpack_kernel(total, kernel_grad, gain_grad, up_grad, bias_grad, down_grad, scale_grad):
    quarters = up_grad.shape[1] // LANES
    units = quarters * LANES
    for q in range(quarters):
        lanes = slice(q * LANES, (q + 1) * LANES)
        up_grad[:, lanes] = total[q * LANES : (q + 1) * LANES, :].astype(f32)
        down_grad[lanes, :] = total[units + q * LANES : units + (q + 1) * LANES, :].astype(f32)
    at = 2 * units
    rest = total[at:, :].astype(f32)
    kernel_grad[...] = rest[0:TAPS]
    scale_grad[...] = rest[TAPS : TAPS + 1]
    gain_grad[...] = rest[TAPS + 1 : TAPS + 2]
    for q in range(quarters):
        row = TAPS + 2 + q
        bias_grad[:, q * LANES : (q + 1) * LANES] = rest[row : row + 1]


def shape(dims, dtype=bf16):
    return jax.ShapeDtypeStruct(dims, dtype)


STRIP = (HALO, TILE, LANES)
WHOLE = (TILE, TILE, LANES)


def call(kernel, scalars, operands, outs, scratch, flops):
    size = sum(math.prod(a.shape) * a.dtype.itemsize for a in (*operands, *outs))
    return pl.pallas_call(
        kernel,
        out_shape=outs,
        in_specs=[SMEM] * len(scalars) + [VMEM] * len(operands),
        out_specs=[VMEM] * len(outs),
        scratch_shapes=scratch,
        compiler_params=pltpu.CompilerParams(vmem_limit_bytes=VMEM_LIMIT),
        cost_estimate=pl.CostEstimate(flops=flops, bytes_accessed=size, transcendentals=0),
    )(*scalars, *operands)


def shifted(value, step):
    count = lax.axis_size(SPACE)
    first, last = (max(0, -step), min(count, count - step))
    return lax.ppermute(value, SPACE, [(source, source + step) for source in range(first, last)])


def exchange(top, bottom, to_before, to_after):
    sent = {3: bottom, 2: bottom, 1: to_after, -1: to_before, -2: top, -3: top}
    return [shifted(sent[-step], -step) for step in STEPS]


def spread(value, axes):
    copies = jnp.broadcast_to(value, (lax.axis_size(axes),) + value.shape)
    return lax.all_to_all(copies, axes, 0, 0, tiled=True)


def local(
    fields,
    cotangent,
    land_mask,
    neighbours,
    conv_kernel,
    norm_gain,
    up_weight,
    up_bias,
    down_weight,
    layer_scale,
):
    beside = neighbours[0]
    where = lax.axis_index(SPACE).astype(jnp.int32)[None]
    tile, upstream = fields[0, 0], cotangent[0, 0]
    mask = jnp.broadcast_to(land_mask[0].astype(bf16)[..., None], WHOLE)
    taps = conv_kernel.reshape(TAPS, LANES)
    units = up_weight.shape[1]
    quarters = units // LANES
    sum_rows = -(-(2 * units + TAPS + 2 + quarters) // 64) * 64

    rims = call(
        pack_kernel,
        (beside, where),
        (tile, mask),
        [shape(STRIP)] * 4,
        [pltpu.VMEM((TILE * TILE, LANES), f32)],
        TILE * TILE * LANES,
    )
    strips = exchange(*rims)
    block_out, conv_grad, *rims, sums = call(
        block_kernel,
        (beside, where),
        (
            tile,
            upstream,
            mask,
            *strips,
            taps,
            norm_gain[None],
            up_weight,
            up_bias[None],
            down_weight,
            layer_scale[None],
        ),
        [shape(WHOLE), shape(WHOLE)] + [shape(STRIP)] * 4 + [shape((sum_rows, LANES), f32)],
        [
            pltpu.VMEM((EXT_ROWS, EXT_COLS, LANES), f32),
            pltpu.VMEM((TILE * TILE, LANES), f32),
            pltpu.VMEM((CELLS_IN_CHUNK, LANES), f32),
            pltpu.VMEM((CELLS_IN_CHUNK, LANES), f32),
            pltpu.VMEM((CELLS_IN_CHUNK, LANES), bf16),
            pltpu.VMEM((CELLS_IN_CHUNK, LANES), bf16),
            pltpu.VMEM((CELLS_IN_CHUNK, units), f32),
            pltpu.VMEM((CELLS_IN_CHUNK, units), f32),
            pltpu.VMEM((CELLS_IN_CHUNK, units), bf16),
            pltpu.VMEM((CELLS_IN_CHUNK, units), bf16),
            pltpu.VMEM((LANES, units), f32),
            pltpu.VMEM((LANES, units), f32),
            pltpu.VMEM((8, units), f32),
            pltpu.VMEM((TAPS, 8, LANES), f32),
            pltpu.VMEM((16, LANES), f32),
        ],
        12 * TILE * TILE * LANES * units,
    )
    strips = exchange(*rims)
    cells = TILE * TILE * lax.axis_size(DP) * lax.axis_size(SPACE)
    part = sums.reshape(lax.axis_size(PLANE), -1, LANES)
    part = jnp.sum(lax.all_to_all(part, PLANE, 0, 0, tiled=True), axis=0)
    part, strips = lax.optimization_barrier((part, strips))
    part = jnp.sum(spread(part, "z"), axis=0) * (1.0 / math.sqrt(cells))
    total = spread(part.astype(bf16), PLANE).reshape(sum_rows, LANES)
    (fields_grad,) = call(
        back_kernel,
        (beside, where),
        (conv_grad, upstream, mask, *strips, taps[::-1]),
        [shape(WHOLE)],
        [pltpu.VMEM((EXT_ROWS, EXT_COLS, LANES), f32)],
        2 * TAPS * TILE * TILE * LANES,
    )
    kernel_grad, gain_grad, up_grad, bias_grad, down_grad, scale_grad = call(
        unpack_kernel,
        (),
        (total,),
        [
            shape((TAPS, LANES), f32),
            shape((1, LANES), f32),
            shape((LANES, units), f32),
            shape((1, units), f32),
            shape((units, LANES), f32),
            shape((1, LANES), f32),
        ],
        [],
        sum_rows * LANES,
    )
    return (
        block_out[None, None],
        fields_grad[None, None],
        kernel_grad.reshape(KERNEL, KERNEL, LANES),
        gain_grad[0],
        up_grad,
        bias_grad[0],
        down_grad,
        scale_grad[0],
    )


def solution(mesh):
    fine = jax.sharding.Mesh(mesh.devices.reshape(2, 4, 2, 16, 2), DP + SPACE)
    tiles = P(DP, SPACE, None, None, None)
    return jax.shard_map(
        local,
        mesh=fine,
        in_specs=(
            tiles,
            tiles,
            P(SPACE, None, None),
            P(SPACE, None),
            P(),
            P(),
            P(),
            P(),
            P(),
            P(),
        ),
        out_specs=(tiles, tiles, P(), P(), P(), P(), P(), P()),
        check_vma=False,
    )
```

```python
import math

import jax
import jax.numpy as jnp
from jax import lax
from jax.experimental import pallas as pl
from jax.experimental.pallas import tpu as pltpu
from jax.sharding import PartitionSpec as P

KERNEL = 7
DILATION = 2
HALO = 6
TAPS = KERNEL * KERNEL
TILE = 48
LANES = 128
PAD = 2
EXT_ROWS = TILE + 2 * HALO
EXT_COLS = 64
CHUNK = 16
CELLS_IN_CHUNK = CHUNK * TILE
GROUPS = TILE // 8
STEPS = (-3, -2, -1, 1, 2, 3)
LARGE, SMALL = 60 * 2**20, 16 * 2**20
DP = ("x_hi", "y", "core")
SPACE = ("z", "x_lo")
PLANE = ("x_hi", "y", "core", "x_lo")

norm_eps = 1e-06
inv_sqrt_two_pi = 0.3989422804014327
TAIL_RATE = 0.3889087296526013
TAIL_TERMS = (
    0.15079174476614957,
    0.19542085643011212,
    -0.02071252121020706,
    0.379856419408137,
    -0.25901857729927547,
    0.05366208632016299,
)

f32 = jnp.float32
bf16 = jnp.bfloat16
VMEM = pl.BlockSpec(memory_space=pltpu.VMEM)
SMEM = pl.BlockSpec(memory_space=pltpu.SMEM)
HBM = pl.BlockSpec(memory_space=pltpu.HBM)


def pack_strips(flat, beside, where, top, bottom, to_before, to_after):
    position = where[0]
    upper = flat[0 : HALO * TILE, :].astype(bf16).reshape(HALO, TILE, LANES)
    lower = flat[(TILE - HALO) * TILE :, :].astype(bf16).reshape(HALO, TILE, LANES)
    top[...] = upper
    bottom[...] = lower
    to_before[...] = upper
    to_after[...] = lower

    def columns(out, first):
        for c in range(HALO):
            parts = [
                flat[pl.ds(8 * g * TILE + first + c, 8, stride=TILE), :] for g in range(GROUPS)
            ]
            out[c] = jnp.concatenate(parts, axis=0).astype(bf16)

    for out, step in ((to_before, -1), (to_after, 1)):
        for direction, first in ((2, 0), (3, TILE - HALO)):
            source = beside[direction]

            @pl.when((source >= 0) & (source - position == step))
            def _(out=out, first=first):
                columns(out, first)


def place_rims(ext, ext_flat, beside, where, strips):
    position = where[0]
    zero_rows = jnp.zeros((HALO, EXT_COLS, LANES), f32)
    zero_cols = jnp.zeros((TILE, 8, LANES), f32)
    ext[0:HALO] = zero_rows
    ext[HALO + TILE :] = zero_rows
    ext[HALO : HALO + TILE, 0:8, :] = zero_cols
    ext[HALO : HALO + TILE, 8 + TILE :, :] = zero_cols
    last = TILE - 8

    def put_rows(first):
        def put(strip):
            ext[first : first + HALO, 8 : 8 + TILE, :] = strip.astype(f32)

        return put

    def put_corner(first, east):
        def put(strip):
            wide = strip.astype(f32)
            if east:
                ext[first : first + HALO, 8 + TILE :, :] = wide[:, 0:8]
            else:
                ext[first : first + HALO, 0:8, :] = wide[:, last:]

        return put

    def put_columns(first):
        def put(strip):
            wide = strip.astype(f32)
            for c in range(HALO):
                for g in range(GROUPS):
                    at = (HALO + 8 * g) * EXT_COLS + first + c
                    ext_flat[pl.ds(at, 8, stride=EXT_COLS), :] = wide[c, 8 * g : 8 * g + 8]

        return put

    south_row = HALO + TILE
    before, after = (-1, -2, -3), (1, 2, 3)
    for direction, steps, put in (
        (4, before, put_corner(0, False)),
        (5, before, put_corner(0, True)),
        (6, after, put_corner(south_row, False)),
        (7, after, put_corner(south_row, True)),
        (0, before, put_rows(0)),
        (1, after, put_rows(south_row)),
        (2, (-1, 1), put_columns(PAD)),
        (3, (-1, 1), put_columns(8 + TILE)),
    ):
        source = beside[direction]
        for step in steps:

            @pl.when((source >= 0) & (source - position == step))
            def _(step=step, put=put):
                put(strips[STEPS.index(step)][...])


def conv_group(ext, weights, first_row, g):
    sums = [None] * CHUNK
    for b in range(KERNEL):
        taps = [
            jnp.broadcast_to(weights[a * KERNEL + b : a * KERNEL + b + 1, :], (8, LANES))
            for a in range(KERNEL)
        ]
        column = PAD + 8 * g + DILATION * b
        for i in range(CHUNK + 2 * HALO):
            window = ext[first_row + i, pl.ds(column, 8), :]
            for a in range(KERNEL):
                row = i - DILATION * a
                if 0 <= row < CHUNK:
                    term = taps[a] * window
                    sums[row] = term if sums[row] is None else sums[row] + term
    return sums


def pack_kernel(beside, where, fields, mask, top, bottom, to_before, to_after, flat):
    def rows(i, _):
        cells = pl.ds(pl.multiple_of(i * TILE, TILE), TILE)
        flat[cells, :] = fields[i].astype(f32) * mask[i].astype(f32)
        return 0

    lax.fori_loop(0, TILE, rows, 0, unroll=4)
    pack_strips(flat, beside, where, top, bottom, to_before, to_after)


def start_copies(sources, targets, done):
    copies = [
        pltpu.make_async_copy(source, target, done.at[i])
        for i, (source, target) in enumerate(zip(sources, targets))
    ]
    for copy in copies:
        copy.start()
    return copies


def block_kernel(
    beside,
    where,
    fields_hbm,
    mask_hbm,
    s0,
    s1,
    s2,
    s3,
    s4,
    s5,
    weights_hbm,
    cotangent_hbm,
    up_weight_hbm,
    down_weight_hbm,
    gain,
    up_bias,
    scale,
    block_out,
    conv_grad,
    top,
    bottom,
    to_before,
    to_after,
    sums,
    ext,
    grad_flat,
    standard,
    inv_std,
    normed,
    branch_grad,
    hidden,
    active_grad,
    active,
    hidden_grad,
    up_sum,
    down_sum,
    bias_sum,
    tap_sums,
    row_sums,
    fields,
    mask,
    strips,
    weights,
    cotangent,
    up_weight,
    down_weight,
    done,
):
    ext_flat = ext.reshape(EXT_ROWS * EXT_COLS, LANES)
    rims = [strips.at[i] for i in range(len(STEPS))]
    copies = start_copies(
        (fields_hbm, mask_hbm, s0, s1, s2, s3, s4, s5)
        + (weights_hbm, cotangent_hbm, up_weight_hbm, down_weight_hbm),
        [fields, mask, *rims, weights, cotangent, up_weight, down_weight],
        done,
    )
    up_sum[...] = jnp.zeros_like(up_sum)
    down_sum[...] = jnp.zeros_like(down_sum)
    bias_sum[...] = jnp.zeros_like(bias_sum)
    tap_sums[...] = jnp.zeros_like(tap_sums)
    row_sums[...] = jnp.zeros_like(row_sums)
    for copy in copies[:2]:
        copy.wait()

    def centre(i, _):
        ext[HALO + i, pl.ds(8, TILE), :] = fields[i].astype(f32) * mask[i].astype(f32)
        return 0

    lax.fori_loop(0, TILE, centre, 0, unroll=4)
    for copy in copies[2:]:
        copy.wait()
    place_rims(ext, ext_flat, beside, where, rims)
    ones = jnp.ones((8, CELLS_IN_CHUNK), bf16)

    def chunk(step, _):
        first = pl.multiple_of(step * CHUNK, CHUNK)
        for g in range(GROUPS):
            values = conv_group(ext, weights, first, g)
            for row in range(CHUNK):
                standard[pl.ds(row * TILE + 8 * g, 8), :] = values[row]

        def normalise(row, _):
            cells = pl.ds(pl.multiple_of(row * TILE, TILE), TILE)
            conv = standard[cells, :]
            centered = conv - jnp.mean(conv, axis=-1, keepdims=True)
            inv = lax.rsqrt(jnp.mean(centered * centered, axis=-1, keepdims=True) + norm_eps)
            unit = centered * inv
            standard[cells, :] = unit
            inv_std[cells, :] = jnp.broadcast_to(inv, (TILE, LANES))
            normed[cells, :] = (unit * gain[...]).astype(bf16)
            weighted = mask[first + row].astype(f32) * scale[...]
            branch_grad[cells, :] = (weighted * cotangent[first + row].astype(f32)).astype(bf16)
            return 0

        lax.fori_loop(0, CHUNK, normalise, 0, unroll=CHUNK)
        hidden[...] = jnp.dot(normed[...], up_weight[...], preferred_element_type=f32)
        active_grad[...] = lax.dot_general(
            branch_grad[...],
            down_weight[...],
            (((1,), (1,)), ((), ())),
            preferred_element_type=f32,
        )

        def activate(i, _):
            cells = pl.ds(pl.multiple_of(i * 16, 16), 16)
            h = hidden[cells, :] + up_bias[...]
            t = pl.reciprocal(1.0 + TAIL_RATE * jnp.abs(h), approx=False)
            tail = TAIL_TERMS[-1] * t + TAIL_TERMS[-2]
            for term in TAIL_TERMS[-3::-1]:
                tail = tail * t + term
            bell = jnp.exp(-0.5 * h * h)
            tail = tail * t * bell
            phi = jnp.where(h >= 0, 1.0 - tail, tail)
            active[cells, :] = (h * phi).astype(bf16)
            slope = phi + h * (bell * inv_sqrt_two_pi)
            hidden_grad[cells, :] = (active_grad[cells, :] * slope).astype(bf16)
            return 0

        lax.fori_loop(0, CELLS_IN_CHUNK // 16, activate, 0, unroll=CELLS_IN_CHUNK // 16)
        hidden[:, 0:LANES] = jnp.dot(active[...], down_weight[...], preferred_element_type=f32)
        active_grad[:, 0:LANES] = lax.dot_general(
            hidden_grad[...], up_weight[...], (((1,), (1,)), ((), ())), preferred_element_type=f32
        )
        over_cells = (((0,), (0,)), ((), ()))
        down_sum[...] += lax.dot_general(
            branch_grad[...], active[...], over_cells, preferred_element_type=f32
        )
        up_sum[...] += lax.dot_general(
            normed[...], hidden_grad[...], over_cells, preferred_element_type=f32
        )
        bias_sum[...] += jnp.dot(ones, hidden_grad[...], preferred_element_type=f32)

        def finish(row, _):
            cells = pl.ds(pl.multiple_of(row * TILE, TILE), TILE)
            at = first + row
            masked_branch = mask[at].astype(f32) * hidden[cells, 0:LANES]
            block_out[at] = (fields[at].astype(f32) + masked_branch * scale[...]).astype(bf16)
            by_scale = masked_branch * cotangent[at].astype(f32)
            unit = standard[cells, :]
            grad = active_grad[cells, 0:LANES]
            by_gain = grad * unit
            u = grad * gain[...]
            mean_u = jnp.mean(u, axis=-1, keepdims=True)
            mean_us = jnp.mean(u * unit, axis=-1, keepdims=True)
            out = (inv_std[cells, :] * (u - mean_u - unit * mean_us)).astype(bf16)
            conv_grad[at] = out
            grad_flat[pl.ds(pl.multiple_of(at * TILE, TILE), TILE), :] = out.astype(f32)
            for k in range(GROUPS):
                row_sums[0:8, :] += by_scale[8 * k : 8 * k + 8]
                row_sums[8:16, :] += by_gain[8 * k : 8 * k + 8]
            return 0

        lax.fori_loop(0, CHUNK, finish, 0, unroll=CHUNK)
        for b in range(KERNEL):
            totals = [tap_sums[a * KERNEL + b] for a in range(KERNEL)]
            for g in range(GROUPS):
                grads = [
                    grad_flat[pl.ds((first + row) * TILE + 8 * g, 8), :] for row in range(CHUNK)
                ]
                column = PAD + 8 * g + DILATION * b
                for i in range(CHUNK + 2 * HALO):
                    window = ext[first + i, pl.ds(column, 8), :]
                    for a in range(KERNEL):
                        row = i - DILATION * a
                        if 0 <= row < CHUNK:
                            totals[a] = totals[a] + grads[row] * window
            for a in range(KERNEL):
                tap_sums[a * KERNEL + b] = totals[a]
        return 0

    lax.fori_loop(0, TILE // CHUNK, chunk, 0)
    pack_strips(grad_flat, beside, where, top, bottom, to_before, to_after)

    quarters = up_sum.shape[1] // LANES
    for q in range(quarters):
        lanes = slice(q * LANES, (q + 1) * LANES)
        sums[q * LANES : (q + 1) * LANES, :] = up_sum[:, lanes]
        sums[(quarters + q) * LANES : (quarters + q + 1) * LANES, :] = down_sum[:, lanes].T
    at = 2 * quarters * LANES
    sums[at:, :] = jnp.zeros((sums.shape[0] - at, LANES), f32)
    sums[at : at + TAPS, :] = jnp.sum(tap_sums[...], axis=1)
    sums[at + TAPS : at + TAPS + 1, :] = jnp.sum(row_sums[0:8, :], axis=0, keepdims=True)
    sums[at + TAPS + 1 : at + TAPS + 2, :] = jnp.sum(row_sums[8:16, :], axis=0, keepdims=True)
    for q in range(quarters):
        row = at + TAPS + 2 + q
        sums[row : row + 1, :] = bias_sum[0:1, q * LANES : (q + 1) * LANES]


def back_kernel(
    beside,
    where,
    conv_grad_hbm,
    s0,
    s1,
    s2,
    s3,
    s4,
    s5,
    weights_hbm,
    mask_hbm,
    cotangent_hbm,
    fields_grad,
    ext,
    conv_grad,
    strips,
    weights,
    mask,
    cotangent,
    done,
):
    ext_flat = ext.reshape(EXT_ROWS * EXT_COLS, LANES)
    rims = [strips.at[i] for i in range(len(STEPS))]
    copies = start_copies(
        (conv_grad_hbm, s0, s1, s2, s3, s4, s5, weights_hbm, mask_hbm, cotangent_hbm),
        [conv_grad, *rims, weights, mask, cotangent],
        done,
    )
    copies[0].wait()

    def centre(i, _):
        ext[HALO + i, pl.ds(8, TILE), :] = conv_grad[i].astype(f32)
        return 0

    lax.fori_loop(0, TILE, centre, 0, unroll=4)
    for copy in copies[1:]:
        copy.wait()
    place_rims(ext, ext_flat, beside, where, rims)

    def chunk(step, _):
        first = pl.multiple_of(step * CHUNK, CHUNK)
        columns = [conv_group(ext, weights, first, g) for g in range(GROUPS)]
        for row in range(CHUNK):
            at = first + row
            whole = jnp.concatenate([columns[g][row] for g in range(GROUPS)], axis=0)
            out = cotangent[at].astype(f32) + mask[at].astype(f32) * whole
            fields_grad[at] = out.astype(bf16)
        return 0

    lax.fori_loop(0, TILE // CHUNK, chunk, 0)


def unpack_kernel(total, kernel_grad, gain_grad, up_grad, bias_grad, down_grad, scale_grad):
    quarters = up_grad.shape[1] // LANES
    units = quarters * LANES
    for q in range(quarters):
        lanes = slice(q * LANES, (q + 1) * LANES)
        up_grad[:, lanes] = total[q * LANES : (q + 1) * LANES, :].astype(f32)
        down_grad[lanes, :] = total[units + q * LANES : units + (q + 1) * LANES, :].astype(f32)
    at = 2 * units
    rest = total[at:, :].astype(f32)
    kernel_grad[...] = rest[0:TAPS]
    scale_grad[...] = rest[TAPS : TAPS + 1]
    gain_grad[...] = rest[TAPS + 1 : TAPS + 2]
    for q in range(quarters):
        row = TAPS + 2 + q
        bias_grad[:, q * LANES : (q + 1) * LANES] = rest[row : row + 1]


def shape(dims, dtype=bf16):
    return jax.ShapeDtypeStruct(dims, dtype)


STRIP = (HALO, TILE, LANES)
WHOLE = (TILE, TILE, LANES)


def call(kernel, scalars, operands, outs, scratch, flops, limit, spaces=VMEM):
    size = sum(math.prod(a.shape) * a.dtype.itemsize for a in (*operands, *outs))
    return pl.pallas_call(
        kernel,
        out_shape=outs,
        in_specs=[SMEM] * len(scalars) + (spaces if spaces is not VMEM else [VMEM] * len(operands)),
        out_specs=[VMEM] * len(outs),
        scratch_shapes=scratch,
        compiler_params=pltpu.CompilerParams(vmem_limit_bytes=limit),
        cost_estimate=pl.CostEstimate(flops=flops, bytes_accessed=size, transcendentals=0),
    )(*scalars, *operands)


def shifted(value, step):
    count = lax.axis_size(SPACE)
    first, last = (max(0, -step), min(count, count - step))
    return lax.ppermute(value, SPACE, [(source, source + step) for source in range(first, last)])


def exchange(top, bottom, to_before, to_after):
    sent = {3: bottom, 2: bottom, 1: to_after, -1: to_before, -2: top, -3: top}
    return [shifted(sent[-step], -step) for step in STEPS]


def spread(value, axes):
    copies = jnp.broadcast_to(value, (lax.axis_size(axes),) + value.shape)
    return lax.all_to_all(copies, axes, 0, 0, tiled=True)


def block_call(beside, where, *operands):
    units = operands[10].shape[1]
    quarters = units // LANES
    sum_rows = -(-(2 * units + TAPS + 2 + quarters) // 64) * 64
    return call(
        block_kernel,
        (beside, where),
        operands,
        [shape(WHOLE), shape(WHOLE)] + [shape(STRIP)] * 4 + [shape((sum_rows, LANES), f32)],
        [
            pltpu.VMEM((EXT_ROWS, EXT_COLS, LANES), f32),
            pltpu.VMEM((TILE * TILE, LANES), f32),
            pltpu.VMEM((CELLS_IN_CHUNK, LANES), f32),
            pltpu.VMEM((CELLS_IN_CHUNK, LANES), f32),
            pltpu.VMEM((CELLS_IN_CHUNK, LANES), bf16),
            pltpu.VMEM((CELLS_IN_CHUNK, LANES), bf16),
            pltpu.VMEM((CELLS_IN_CHUNK, units), f32),
            pltpu.VMEM((CELLS_IN_CHUNK, units), f32),
            pltpu.VMEM((CELLS_IN_CHUNK, units), bf16),
            pltpu.VMEM((CELLS_IN_CHUNK, units), bf16),
            pltpu.VMEM((LANES, units), f32),
            pltpu.VMEM((LANES, units), f32),
            pltpu.VMEM((8, units), f32),
            pltpu.VMEM((TAPS, 8, LANES), f32),
            pltpu.VMEM((16, LANES), f32),
            pltpu.VMEM(WHOLE, bf16),
            pltpu.VMEM(WHOLE, bf16),
            pltpu.VMEM((len(STEPS), *STRIP), bf16),
            pltpu.VMEM((TAPS, LANES), f32),
            pltpu.VMEM(WHOLE, bf16),
            pltpu.VMEM((LANES, units), bf16),
            pltpu.VMEM((units, LANES), bf16),
            pltpu.SemaphoreType.DMA((12,)),
        ],
        12 * TILE * TILE * LANES * units,
        LARGE,
        [HBM] * 12 + [VMEM] * 3,
    )


def local(
    fields,
    cotangent,
    land_mask,
    neighbours,
    conv_kernel,
    norm_gain,
    up_weight,
    up_bias,
    down_weight,
    layer_scale,
):
    beside = neighbours[0]
    where = lax.axis_index(SPACE).astype(jnp.int32)[None]
    tile, upstream = fields[0, 0], cotangent[0, 0]
    mask = jnp.broadcast_to(land_mask[0].astype(bf16)[..., None], WHOLE)
    taps = conv_kernel.reshape(TAPS, LANES)
    units = up_weight.shape[1]

    rims = call(
        pack_kernel,
        (beside, where),
        (tile, mask),
        [shape(STRIP)] * 4,
        [pltpu.VMEM((TILE * TILE, LANES), f32)],
        TILE * TILE * LANES,
        SMALL,
    )
    strips = exchange(*rims)
    block_out, conv_grad, *rims, sums = block_call(
        beside,
        where,
        tile,
        mask,
        *strips,
        taps,
        upstream,
        up_weight,
        down_weight,
        norm_gain[None],
        up_bias[None],
        layer_scale[None],
    )
    sum_rows = sums.shape[0]
    cells = TILE * TILE * lax.axis_size(DP) * lax.axis_size(SPACE)
    part = sums.reshape(lax.axis_size(PLANE), -1, LANES)
    part = jnp.sum(lax.all_to_all(part, PLANE, 0, 0, tiled=True), axis=0)
    part, rims = lax.optimization_barrier((part, rims))
    strips = exchange(*rims)
    part = jnp.sum(spread(part, "z"), axis=0) * (1.0 / math.sqrt(cells))
    part, strips = lax.optimization_barrier((part, strips))
    total = spread(part.astype(bf16), PLANE).reshape(sum_rows, LANES)
    (fields_grad,) = call(
        back_kernel,
        (beside, where),
        (conv_grad, *strips, taps[::-1], mask, upstream),
        [shape(WHOLE)],
        [
            pltpu.VMEM((EXT_ROWS, EXT_COLS, LANES), f32),
            pltpu.VMEM(WHOLE, bf16),
            pltpu.VMEM((len(STEPS), *STRIP), bf16),
            pltpu.VMEM((TAPS, LANES), f32),
            pltpu.VMEM(WHOLE, bf16),
            pltpu.VMEM(WHOLE, bf16),
            pltpu.SemaphoreType.DMA((10,)),
        ],
        2 * TAPS * TILE * TILE * LANES,
        LARGE,
        [HBM] * 10,
    )
    total, fields_grad = lax.optimization_barrier((total, fields_grad))
    kernel_grad, gain_grad, up_grad, bias_grad, down_grad, scale_grad = call(
        unpack_kernel,
        (),
        (total,),
        [
            shape((TAPS, LANES), f32),
            shape((1, LANES), f32),
            shape((LANES, units), f32),
            shape((1, units), f32),
            shape((units, LANES), f32),
            shape((1, LANES), f32),
        ],
        [],
        sum_rows * LANES,
        SMALL,
    )
    return (
        block_out[None, None],
        fields_grad[None, None],
        kernel_grad.reshape(KERNEL, KERNEL, LANES),
        gain_grad[0],
        up_grad,
        bias_grad[0],
        down_grad,
        scale_grad[0],
    )


def solution(mesh):
    fine = jax.sharding.Mesh(mesh.devices.reshape(2, 4, 2, 16, 2), DP + SPACE)
    tiles = P(DP, SPACE, None, None, None)
    return jax.shard_map(
        local,
        mesh=fine,
        in_specs=(
            tiles,
            tiles,
            P(SPACE, None, None),
            P(SPACE, None),
            P(),
            P(),
            P(),
            P(),
            P(),
            P(),
        ),
        out_specs=(tiles, tiles, P(), P(), P(), P(), P(), P()),
        check_vma=False,
    )
```

```python
import math

import jax
import jax.numpy as jnp
from jax import lax
from jax.experimental import pallas as pl
from jax.experimental.pallas import tpu as pltpu
from jax.sharding import PartitionSpec as P

KERNEL = 7
DILATION = 2
HALO = 6
TAPS = KERNEL * KERNEL
TILE = 48
LANES = 128
PAD = 2
EXT_ROWS = TILE + 2 * HALO
EXT_COLS = 64
CHUNK = 16
CELLS_IN_CHUNK = CHUNK * TILE
GROUPS = TILE // 8
STEPS = (-3, -2, -1, 1, 2, 3)
LARGE, SMALL = 60 * 2**20, 16 * 2**20
DP = ("x_hi", "y", "core")
SPACE = ("z", "x_lo")
PLANE = ("x_hi", "y", "core", "x_lo")

SHARES = 32 * 8

norm_eps = 1e-06
inv_sqrt_two_pi = 0.3989422804014327
TAIL_RATE = 0.3889087296526013
TAIL_TERMS = (
    0.15079174476614957,
    0.19542085643011212,
    -0.02071252121020706,
    0.379856419408137,
    -0.25901857729927547,
    0.05366208632016299,
)

f32 = jnp.float32
bf16 = jnp.bfloat16
VMEM = pl.BlockSpec(memory_space=pltpu.VMEM)
SMEM = pl.BlockSpec(memory_space=pltpu.SMEM)
HBM = pl.BlockSpec(memory_space=pltpu.HBM)


def pack_strips(flat, beside, where, top, bottom, to_before, to_after):
    position = where[0]
    upper = flat[0 : HALO * TILE, :].astype(bf16).reshape(HALO, TILE, LANES)
    lower = flat[(TILE - HALO) * TILE :, :].astype(bf16).reshape(HALO, TILE, LANES)
    top[...] = upper
    bottom[...] = lower
    to_before[...] = upper
    to_after[...] = lower

    def columns(out, first):
        for c in range(HALO):
            parts = [
                flat[pl.ds(8 * g * TILE + first + c, 8, stride=TILE), :] for g in range(GROUPS)
            ]
            out[c] = jnp.concatenate(parts, axis=0).astype(bf16)

    for out, step in ((to_before, -1), (to_after, 1)):
        for direction, first in ((2, 0), (3, TILE - HALO)):
            source = beside[0, direction]

            @pl.when((source >= 0) & (source - position == step))
            def _(out=out, first=first):
                columns(out, first)


def place_rims(ext, ext_flat, beside, where, strips):
    position = where[0]
    zero_rows = jnp.zeros((HALO, EXT_COLS, LANES), f32)
    zero_cols = jnp.zeros((TILE, 8, LANES), f32)
    ext[0:HALO] = zero_rows
    ext[HALO + TILE :] = zero_rows
    ext[HALO : HALO + TILE, 0:8, :] = zero_cols
    ext[HALO : HALO + TILE, 8 + TILE :, :] = zero_cols
    last = TILE - 8

    def put_rows(first):
        def put(strip):
            ext[first : first + HALO, 8 : 8 + TILE, :] = strip.astype(f32)

        return put

    def put_corner(first, east):
        def put(strip):
            wide = strip.astype(f32)
            if east:
                ext[first : first + HALO, 8 + TILE :, :] = wide[:, 0:8]
            else:
                ext[first : first + HALO, 0:8, :] = wide[:, last:]

        return put

    def put_columns(first):
        def put(strip):
            wide = strip.astype(f32)
            for c in range(HALO):
                for g in range(GROUPS):
                    at = (HALO + 8 * g) * EXT_COLS + first + c
                    ext_flat[pl.ds(at, 8, stride=EXT_COLS), :] = wide[c, 8 * g : 8 * g + 8]

        return put

    south_row = HALO + TILE
    before, after = (-1, -2, -3), (1, 2, 3)
    for direction, steps, put in (
        (4, before, put_corner(0, False)),
        (5, before, put_corner(0, True)),
        (6, after, put_corner(south_row, False)),
        (7, after, put_corner(south_row, True)),
        (0, before, put_rows(0)),
        (1, after, put_rows(south_row)),
        (2, (-1, 1), put_columns(PAD)),
        (3, (-1, 1), put_columns(8 + TILE)),
    ):
        source = beside[0, direction]
        for step in steps:

            @pl.when((source >= 0) & (source - position == step))
            def _(step=step, put=put):
                put(strips[STEPS.index(step)][...])


def conv_group(ext, weights, first_row, g, reverse=False):
    def tap(a, b):
        return (KERNEL - 1 - a, KERNEL - 1 - b) if reverse else (a, b)

    sums = [None] * CHUNK
    for b in range(KERNEL):
        taps = [
            jnp.broadcast_to(weights[tap(a, b)[0], pl.ds(tap(a, b)[1], 1), :], (8, LANES))
            for a in range(KERNEL)
        ]
        column = PAD + 8 * g + DILATION * b
        for i in range(CHUNK + 2 * HALO):
            window = ext[first_row + i, pl.ds(column, 8), :]
            for a in range(KERNEL):
                row = i - DILATION * a
                if 0 <= row < CHUNK:
                    term = taps[a] * window
                    sums[row] = term if sums[row] is None else sums[row] + term
    return sums


def pack_kernel(beside, where, land_mask, fields, mask, top, bottom, to_before, to_after, flat):
    side = (TILE, TILE)
    diagonal = lax.broadcasted_iota(jnp.int32, side, 0) == lax.broadcasted_iota(jnp.int32, side, 1)
    by_column = lax.dot_general(
        land_mask[0].astype(f32).astype(bf16),
        jnp.where(diagonal, 1.0, 0.0).astype(bf16),
        (((0,), (0,)), ((), ())),
        preferred_element_type=f32,
    )
    for row in range(TILE):
        wide = jnp.broadcast_to(by_column[:, row : row + 1], (TILE, LANES))
        mask[row] = wide.astype(bf16)
        flat[row * TILE : (row + 1) * TILE, :] = fields[0, 0, row].astype(f32) * wide
    pack_strips(flat, beside, where, top, bottom, to_before, to_after)


def start_copies(sources, targets, done):
    copies = [
        pltpu.make_async_copy(source, target, done.at[i])
        for i, (source, target) in enumerate(zip(sources, targets))
    ]
    for copy in copies:
        copy.start()
    return copies


def block_kernel(
    beside,
    where,
    fields_hbm,
    mask_hbm,
    s0,
    s1,
    s2,
    s3,
    s4,
    s5,
    weights_hbm,
    cotangent_hbm,
    up_weight_hbm,
    down_weight_hbm,
    gain,
    up_bias,
    scale,
    block_out,
    conv_grad,
    top,
    bottom,
    to_before,
    to_after,
    sums,
    ext,
    grad_flat,
    standard,
    inv_std,
    normed,
    branch_grad,
    hidden,
    active_grad,
    active,
    hidden_grad,
    up_sum,
    down_sum,
    bias_sum,
    tap_sums,
    row_sums,
    fields,
    mask,
    strips,
    weights,
    cotangent,
    up_weight,
    down_weight,
    done,
):
    ext_flat = ext.reshape(EXT_ROWS * EXT_COLS, LANES)
    rims = [strips.at[i] for i in range(len(STEPS))]
    copies = start_copies(
        (fields_hbm, mask_hbm, s0, s1, s2, s3, s4, s5)
        + (weights_hbm, cotangent_hbm, up_weight_hbm, down_weight_hbm),
        [fields, mask, *rims, weights, cotangent, up_weight, down_weight],
        done,
    )
    up_sum[...] = jnp.zeros_like(up_sum)
    down_sum[...] = jnp.zeros_like(down_sum)
    bias_sum[...] = jnp.zeros_like(bias_sum)
    tap_sums[...] = jnp.zeros_like(tap_sums)
    row_sums[...] = jnp.zeros_like(row_sums)
    for copy in copies[:2]:
        copy.wait()

    def centre(i, _):
        ext[HALO + i, pl.ds(8, TILE), :] = fields[i].astype(f32) * mask[i].astype(f32)
        return 0

    lax.fori_loop(0, TILE, centre, 0, unroll=4)
    for copy in copies[2:]:
        copy.wait()
    place_rims(ext, ext_flat, beside, where, rims)
    ones = jnp.ones((8, CELLS_IN_CHUNK), bf16)

    def chunk(step, _):
        first = pl.multiple_of(step * CHUNK, CHUNK)
        for g in range(GROUPS):
            values = conv_group(ext, weights, first, g)
            for row in range(CHUNK):
                standard[pl.ds(row * TILE + 8 * g, 8), :] = values[row]

        def normalise(row, _):
            cells = pl.ds(pl.multiple_of(row * TILE, TILE), TILE)
            conv = standard[cells, :]
            centered = conv - jnp.mean(conv, axis=-1, keepdims=True)
            inv = lax.rsqrt(jnp.mean(centered * centered, axis=-1, keepdims=True) + norm_eps)
            unit = centered * inv
            standard[cells, :] = unit
            inv_std[cells, :] = jnp.broadcast_to(inv, (TILE, LANES))
            normed[cells, :] = (unit * gain[...]).astype(bf16)
            weighted = mask[first + row].astype(f32) * scale[...]
            branch_grad[cells, :] = (weighted * cotangent[first + row].astype(f32)).astype(bf16)
            return 0

        lax.fori_loop(0, CHUNK, normalise, 0, unroll=CHUNK)
        hidden[...] = jnp.dot(normed[...], up_weight[...], preferred_element_type=f32)
        active_grad[...] = lax.dot_general(
            branch_grad[...],
            down_weight[...],
            (((1,), (1,)), ((), ())),
            preferred_element_type=f32,
        )

        def activate(i, _):
            cells = pl.ds(pl.multiple_of(i * 16, 16), 16)
            h = hidden[cells, :] + up_bias[...]
            t = pl.reciprocal(1.0 + TAIL_RATE * jnp.abs(h), approx=False)
            tail = TAIL_TERMS[-1] * t + TAIL_TERMS[-2]
            for term in TAIL_TERMS[-3::-1]:
                tail = tail * t + term
            bell = jnp.exp(-0.5 * h * h)
            tail = tail * t * bell
            phi = jnp.where(h >= 0, 1.0 - tail, tail)
            active[cells, :] = (h * phi).astype(bf16)
            slope = phi + h * (bell * inv_sqrt_two_pi)
            hidden_grad[cells, :] = (active_grad[cells, :] * slope).astype(bf16)
            return 0

        lax.fori_loop(0, CELLS_IN_CHUNK // 16, activate, 0, unroll=CELLS_IN_CHUNK // 16)
        hidden[:, 0:LANES] = jnp.dot(active[...], down_weight[...], preferred_element_type=f32)
        active_grad[:, 0:LANES] = lax.dot_general(
            hidden_grad[...], up_weight[...], (((1,), (1,)), ((), ())), preferred_element_type=f32
        )
        over_cells = (((0,), (0,)), ((), ()))
        down_sum[...] += lax.dot_general(
            branch_grad[...], active[...], over_cells, preferred_element_type=f32
        )
        up_sum[...] += lax.dot_general(
            normed[...], hidden_grad[...], over_cells, preferred_element_type=f32
        )
        bias_sum[...] += jnp.dot(ones, hidden_grad[...], preferred_element_type=f32)

        def finish(row, _):
            cells = pl.ds(pl.multiple_of(row * TILE, TILE), TILE)
            at = first + row
            masked_branch = mask[at].astype(f32) * hidden[cells, 0:LANES]
            block_out[at] = (fields[at].astype(f32) + masked_branch * scale[...]).astype(bf16)
            by_scale = masked_branch * cotangent[at].astype(f32)
            unit = standard[cells, :]
            grad = active_grad[cells, 0:LANES]
            by_gain = grad * unit
            u = grad * gain[...]
            mean_u = jnp.mean(u, axis=-1, keepdims=True)
            mean_us = jnp.mean(u * unit, axis=-1, keepdims=True)
            out = (inv_std[cells, :] * (u - mean_u - unit * mean_us)).astype(bf16)
            conv_grad[at] = out
            grad_flat[pl.ds(pl.multiple_of(at * TILE, TILE), TILE), :] = out.astype(f32)
            for k in range(GROUPS):
                row_sums[0:8, :] += by_scale[8 * k : 8 * k + 8]
                row_sums[8:16, :] += by_gain[8 * k : 8 * k + 8]
            return 0

        lax.fori_loop(0, CHUNK, finish, 0, unroll=CHUNK)
        for b in range(KERNEL):
            totals = [tap_sums[a * KERNEL + b] for a in range(KERNEL)]
            for g in range(GROUPS):
                grads = [
                    grad_flat[pl.ds((first + row) * TILE + 8 * g, 8), :] for row in range(CHUNK)
                ]
                column = PAD + 8 * g + DILATION * b
                for i in range(CHUNK + 2 * HALO):
                    window = ext[first + i, pl.ds(column, 8), :]
                    for a in range(KERNEL):
                        row = i - DILATION * a
                        if 0 <= row < CHUNK:
                            totals[a] = totals[a] + grads[row] * window
            for a in range(KERNEL):
                tap_sums[a * KERNEL + b] = totals[a]
        return 0

    lax.fori_loop(0, TILE // CHUNK, chunk, 0)
    pack_strips(grad_flat, beside, where, top, bottom, to_before, to_after)

    quarters = up_sum.shape[1] // LANES
    for q in range(quarters):
        lanes = slice(q * LANES, (q + 1) * LANES)
        sums[q * LANES : (q + 1) * LANES, :] = up_sum[:, lanes]
        sums[(quarters + q) * LANES : (quarters + q + 1) * LANES, :] = down_sum[:, lanes].T
    at = 2 * quarters * LANES
    sums[at:, :] = jnp.zeros((sums.shape[0] - at, LANES), f32)
    sums[at : at + TAPS, :] = jnp.sum(tap_sums[...], axis=1)
    sums[at + TAPS : at + TAPS + 1, :] = jnp.sum(row_sums[0:8, :], axis=0, keepdims=True)
    sums[at + TAPS + 1 : at + TAPS + 2, :] = jnp.sum(row_sums[8:16, :], axis=0, keepdims=True)
    for q in range(quarters):
        row = at + TAPS + 2 + q
        sums[row : row + 1, :] = bias_sum[0:1, q * LANES : (q + 1) * LANES]


def back_kernel(
    beside,
    where,
    conv_grad_hbm,
    s0,
    s1,
    s2,
    s3,
    s4,
    s5,
    weights_hbm,
    mask_hbm,
    cotangent_hbm,
    fields_grad,
    ext,
    conv_grad,
    strips,
    weights,
    mask,
    cotangent,
    done,
):
    ext_flat = ext.reshape(EXT_ROWS * EXT_COLS, LANES)
    rims = [strips.at[i] for i in range(len(STEPS))]
    copies = start_copies(
        (conv_grad_hbm, s0, s1, s2, s3, s4, s5, weights_hbm, mask_hbm, cotangent_hbm),
        [conv_grad, *rims, weights, mask, cotangent],
        done,
    )
    copies[0].wait()

    def centre(i, _):
        ext[HALO + i, pl.ds(8, TILE), :] = conv_grad[i].astype(f32)
        return 0

    lax.fori_loop(0, TILE, centre, 0, unroll=4)
    for copy in copies[1:]:
        copy.wait()
    place_rims(ext, ext_flat, beside, where, rims)

    def chunk(step, _):
        first = pl.multiple_of(step * CHUNK, CHUNK)
        columns = [conv_group(ext, weights, first, g, True) for g in range(GROUPS)]
        for row in range(CHUNK):
            at = first + row
            whole = jnp.concatenate([columns[g][row] for g in range(GROUPS)], axis=0)
            out = cotangent[at].astype(f32) + mask[at].astype(f32) * whole
            fields_grad[at] = out.astype(bf16)
        return 0

    lax.fori_loop(0, TILE // CHUNK, chunk, 0)


def unpack_kernel(total, kernel_grad, gain_grad, up_grad, bias_grad, down_grad, scale_grad):
    quarters = up_grad.shape[1] // LANES
    units = quarters * LANES
    for q in range(quarters):
        lanes = slice(q * LANES, (q + 1) * LANES)
        up_grad[:, lanes] = total[q * LANES : (q + 1) * LANES, :].astype(f32)
        down_grad[lanes, :] = total[units + q * LANES : units + (q + 1) * LANES, :].astype(f32)
    at = 2 * units
    rest = total[at : at + 64, :].astype(f32)
    for a in range(KERNEL):
        kernel_grad[a] = rest[a * KERNEL : (a + 1) * KERNEL]
    scale_grad[...] = rest[TAPS : TAPS + 1]
    gain_grad[...] = rest[TAPS + 1 : TAPS + 2]
    for q in range(quarters):
        row = TAPS + 2 + q
        bias_grad[:, q * LANES : (q + 1) * LANES] = rest[row : row + 1]


def shape(dims, dtype=bf16):
    return jax.ShapeDtypeStruct(dims, dtype)


STRIP = (HALO, TILE, LANES)
WHOLE = (TILE, TILE, LANES)


def call(kernel, scalars, operands, outs, scratch, flops, limit, spaces=VMEM):
    size = sum(math.prod(a.shape) * a.dtype.itemsize for a in (*operands, *outs))
    return pl.pallas_call(
        kernel,
        out_shape=outs,
        in_specs=[SMEM] * len(scalars) + (spaces if spaces is not VMEM else [VMEM] * len(operands)),
        out_specs=[VMEM] * len(outs),
        scratch_shapes=scratch,
        compiler_params=pltpu.CompilerParams(vmem_limit_bytes=limit),
        cost_estimate=pl.CostEstimate(flops=flops, bytes_accessed=size, transcendentals=0),
    )(*scalars, *operands)


def shifted(value, step):
    count = lax.axis_size(SPACE)
    first, last = (max(0, -step), min(count, count - step))
    return lax.ppermute(value, SPACE, [(source, source + step) for source in range(first, last)])


def exchange(top, bottom, to_before, to_after, steps=STEPS):
    sent = {3: bottom, 2: bottom, 1: to_after, -1: to_before, -2: top, -3: top}
    return {step: shifted(sent[-step], -step) for step in steps}


def spread(value, axes):
    copies = jnp.broadcast_to(value, (lax.axis_size(axes),) + value.shape)
    return lax.all_to_all(copies, axes, 0, 0, tiled=True)


def block_call(beside, where, *operands):
    units = operands[10].shape[1]
    quarters = units // LANES
    sum_rows = -(-(2 * units + TAPS + 2 + quarters) // SHARES) * SHARES
    return call(
        block_kernel,
        (beside, where),
        operands,
        [shape(WHOLE), shape(WHOLE)] + [shape(STRIP)] * 4 + [shape((sum_rows, LANES), f32)],
        [
            pltpu.VMEM((EXT_ROWS, EXT_COLS, LANES), f32),
            pltpu.VMEM((TILE * TILE, LANES), f32),
            pltpu.VMEM((CELLS_IN_CHUNK, LANES), f32),
            pltpu.VMEM((CELLS_IN_CHUNK, LANES), f32),
            pltpu.VMEM((CELLS_IN_CHUNK, LANES), bf16),
            pltpu.VMEM((CELLS_IN_CHUNK, LANES), bf16),
            pltpu.VMEM((CELLS_IN_CHUNK, units), f32),
            pltpu.VMEM((CELLS_IN_CHUNK, units), f32),
            pltpu.VMEM((CELLS_IN_CHUNK, units), bf16),
            pltpu.VMEM((CELLS_IN_CHUNK, units), bf16),
            pltpu.VMEM((LANES, units), f32),
            pltpu.VMEM((LANES, units), f32),
            pltpu.VMEM((8, units), f32),
            pltpu.VMEM((TAPS, 8, LANES), f32),
            pltpu.VMEM((16, LANES), f32),
            pltpu.VMEM(WHOLE, bf16),
            pltpu.VMEM(WHOLE, bf16),
            pltpu.VMEM((len(STEPS), *STRIP), bf16),
            pltpu.VMEM((KERNEL, KERNEL, LANES), f32),
            pltpu.VMEM(WHOLE, bf16),
            pltpu.VMEM((LANES, units), bf16),
            pltpu.VMEM((units, LANES), bf16),
            pltpu.SemaphoreType.DMA((12,)),
        ],
        12 * TILE * TILE * LANES * units,
        LARGE,
        [HBM] * 12 + [VMEM] * 3,
    )


def local(
    fields,
    cotangent,
    land_mask,
    neighbours,
    conv_kernel,
    norm_gain,
    up_weight,
    up_bias,
    down_weight,
    layer_scale,
):
    beside = neighbours
    where = lax.axis_index(SPACE).astype(jnp.int32)[None]
    tile, upstream = fields[0, 0], cotangent[0, 0]
    units = up_weight.shape[1]
    mask, *rims = call(
        pack_kernel,
        (beside, where),
        (land_mask, fields),
        [shape(WHOLE)] + [shape(STRIP)] * 4,
        [pltpu.VMEM((TILE * TILE, LANES), f32)],
        TILE * TILE * LANES,
        LARGE,
    )
    strips = exchange(*rims)
    strips = [strips[step] for step in STEPS]
    block_out, conv_grad, *rims, sums = block_call(
        beside,
        where,
        tile,
        mask,
        *strips,
        conv_kernel,
        upstream,
        up_weight,
        down_weight,
        norm_gain[None],
        up_bias[None],
        layer_scale[None],
    )
    sum_rows = sums.shape[0]
    cells = TILE * TILE * lax.axis_size(DP) * lax.axis_size(SPACE)
    part = sums.reshape(lax.axis_size(PLANE), -1, LANES)
    part = jnp.sum(lax.all_to_all(part, PLANE, 0, 0, tiled=True), axis=0)
    near = exchange(*rims, steps=(-1, 1))
    part, rims, near = lax.optimization_barrier((part, rims, near))
    far = exchange(*rims, steps=(-3, -2, 2, 3))
    part = jnp.sum(spread(part, "z"), axis=0) * (1.0 / math.sqrt(cells))
    part, far = lax.optimization_barrier((part, far))
    strips = [{**near, **far}[step] for step in STEPS]
    total = spread(part.astype(bf16), PLANE).reshape(sum_rows, LANES)
    (fields_grad,) = call(
        back_kernel,
        (beside, where),
        (conv_grad, *strips, conv_kernel, mask, upstream),
        [shape(WHOLE)],
        [
            pltpu.VMEM((EXT_ROWS, EXT_COLS, LANES), f32),
            pltpu.VMEM(WHOLE, bf16),
            pltpu.VMEM((len(STEPS), *STRIP), bf16),
            pltpu.VMEM((KERNEL, KERNEL, LANES), f32),
            pltpu.VMEM(WHOLE, bf16),
            pltpu.VMEM(WHOLE, bf16),
            pltpu.SemaphoreType.DMA((10,)),
        ],
        2 * TAPS * TILE * TILE * LANES,
        LARGE,
        [HBM] * 10,
    )
    total, fields_grad = lax.optimization_barrier((total, fields_grad))
    kernel_grad, gain_grad, up_grad, bias_grad, down_grad, scale_grad = call(
        unpack_kernel,
        (),
        (total,),
        [
            shape((KERNEL, KERNEL, LANES), f32),
            shape((1, LANES), f32),
            shape((LANES, units), f32),
            shape((1, units), f32),
            shape((units, LANES), f32),
            shape((1, LANES), f32),
        ],
        [],
        sum_rows * LANES,
        SMALL,
    )
    return (
        block_out[None, None],
        fields_grad[None, None],
        kernel_grad,
        gain_grad[0],
        up_grad,
        bias_grad[0],
        down_grad,
        scale_grad[0],
    )


def solution(mesh):
    fine = jax.sharding.Mesh(mesh.devices.reshape(2, 4, 2, 16, 2), DP + SPACE)
    tiles = P(DP, SPACE, None, None, None)
    return jax.shard_map(
        local,
        mesh=fine,
        in_specs=(
            tiles,
            tiles,
            P(SPACE, None, None),
            P(SPACE, None),
            P(),
            P(),
            P(),
            P(),
            P(),
            P(),
        ),
        out_specs=(tiles, tiles, P(), P(), P(), P(), P(), P()),
        check_vma=False,
    )
```

```python
import math

import jax
import jax.numpy as jnp
from jax import lax
from jax.experimental import pallas as pl
from jax.experimental.pallas import tpu as pltpu
from jax.sharding import PartitionSpec as P

KERNEL = 7
DILATION = 2
HALO = 6
TAPS = KERNEL * KERNEL
TILE = 48
LANES = 128
PAD = 2
EXT_ROWS = TILE + 2 * HALO
EXT_COLS = 64
CHUNK = 16
CELLS_IN_CHUNK = CHUNK * TILE
GROUPS = TILE // 8
STEPS = (-3, -2, -1, 1, 2, 3)
LARGE, SMALL = 60 * 2**20, 16 * 2**20
DP = ("x_hi", "y", "core")
SPACE = ("z", "x_lo")
PLANE = ("x_hi", "y", "core", "x_lo")

SHARES = 32 * 8

norm_eps = 1e-06
inv_sqrt_two_pi = 0.3989422804014327
TAIL_RATE = 0.3889087296526013
TAIL_TERMS = (
    0.15079174476614957,
    0.19542085643011212,
    -0.02071252121020706,
    0.379856419408137,
    -0.25901857729927547,
    0.05366208632016299,
)

f32 = jnp.float32
bf16 = jnp.bfloat16
VMEM = pl.BlockSpec(memory_space=pltpu.VMEM)
SMEM = pl.BlockSpec(memory_space=pltpu.SMEM)
HBM = pl.BlockSpec(memory_space=pltpu.HBM)


def pack_strips(flat, beside, where, top, bottom, to_before, to_after):
    position = where[0]
    upper = flat[0 : HALO * TILE, :].astype(bf16).reshape(HALO, TILE, LANES)
    lower = flat[(TILE - HALO) * TILE :, :].astype(bf16).reshape(HALO, TILE, LANES)
    top[...] = upper
    bottom[...] = lower
    to_before[...] = upper
    to_after[...] = lower

    def columns(out, first):
        for c in range(HALO):
            parts = [
                flat[pl.ds(8 * g * TILE + first + c, 8, stride=TILE), :] for g in range(GROUPS)
            ]
            out[c] = jnp.concatenate(parts, axis=0).astype(bf16)

    for out, step in ((to_before, -1), (to_after, 1)):
        for direction, first in ((2, 0), (3, TILE - HALO)):
            source = beside[0, direction]

            @pl.when((source >= 0) & (source - position == step))
            def _(out=out, first=first):
                columns(out, first)


def place_rims(ext, ext_flat, beside, where, strips):
    position = where[0]
    zero_rows = jnp.zeros((HALO, EXT_COLS, LANES), f32)
    zero_cols = jnp.zeros((TILE, 8, LANES), f32)
    ext[0:HALO] = zero_rows
    ext[HALO + TILE :] = zero_rows
    ext[HALO : HALO + TILE, 0:8, :] = zero_cols
    ext[HALO : HALO + TILE, 8 + TILE :, :] = zero_cols
    last = TILE - 8

    def put_rows(first):
        def put(strip):
            ext[first : first + HALO, 8 : 8 + TILE, :] = strip.astype(f32)

        return put

    def put_corner(first, east):
        def put(strip):
            wide = strip.astype(f32)
            if east:
                ext[first : first + HALO, 8 + TILE :, :] = wide[:, 0:8]
            else:
                ext[first : first + HALO, 0:8, :] = wide[:, last:]

        return put

    def put_columns(first):
        def put(strip):
            wide = strip.astype(f32)
            for c in range(HALO):
                for g in range(GROUPS):
                    at = (HALO + 8 * g) * EXT_COLS + first + c
                    ext_flat[pl.ds(at, 8, stride=EXT_COLS), :] = wide[c, 8 * g : 8 * g + 8]

        return put

    south_row = HALO + TILE
    before, after = (-1, -2, -3), (1, 2, 3)
    for direction, steps, put in (
        (4, before, put_corner(0, False)),
        (5, before, put_corner(0, True)),
        (6, after, put_corner(south_row, False)),
        (7, after, put_corner(south_row, True)),
        (0, before, put_rows(0)),
        (1, after, put_rows(south_row)),
        (2, (-1, 1), put_columns(PAD)),
        (3, (-1, 1), put_columns(8 + TILE)),
    ):
        source = beside[0, direction]
        for step in steps:

            @pl.when((source >= 0) & (source - position == step))
            def _(step=step, put=put):
                put(strips[STEPS.index(step)][...])


def conv_group(ext, weights, first_row, g, reverse=False):
    def tap(a, b):
        return (KERNEL - 1 - a, KERNEL - 1 - b) if reverse else (a, b)

    sums = [None] * CHUNK
    for b in range(KERNEL):
        taps = [
            jnp.broadcast_to(weights[tap(a, b)[0], pl.ds(tap(a, b)[1], 1), :], (8, LANES))
            for a in range(KERNEL)
        ]
        column = PAD + 8 * g + DILATION * b
        for i in range(CHUNK + 2 * HALO):
            window = ext[first_row + i, pl.ds(column, 8), :]
            for a in range(KERNEL):
                row = i - DILATION * a
                if 0 <= row < CHUNK:
                    term = taps[a] * window
                    sums[row] = term if sums[row] is None else sums[row] + term
    return sums


def pack_kernel(beside, where, land_mask, fields, mask, top, bottom, to_before, to_after, flat):
    side = (TILE, TILE)
    diagonal = lax.broadcasted_iota(jnp.int32, side, 0) == lax.broadcasted_iota(jnp.int32, side, 1)
    by_column = lax.dot_general(
        land_mask[0].astype(f32).astype(bf16),
        jnp.where(diagonal, 1.0, 0.0).astype(bf16),
        (((0,), (0,)), ((), ())),
        preferred_element_type=f32,
    )
    for row in range(TILE):
        wide = jnp.broadcast_to(by_column[:, row : row + 1], (TILE, LANES))
        mask[row] = wide.astype(bf16)
        flat[row * TILE : (row + 1) * TILE, :] = fields[0, 0, row].astype(f32) * wide
    pack_strips(flat, beside, where, top, bottom, to_before, to_after)


def start_copies(sources, targets, done):
    copies = [
        pltpu.make_async_copy(source, target, done.at[i])
        for i, (source, target) in enumerate(zip(sources, targets))
    ]
    for copy in copies:
        copy.start()
    return copies


def block_kernel(
    beside,
    where,
    fields_hbm,
    mask_hbm,
    s0,
    s1,
    s2,
    s3,
    s4,
    s5,
    weights_hbm,
    cotangent_hbm,
    up_weight_hbm,
    down_weight_hbm,
    gain,
    up_bias,
    scale,
    block_out,
    conv_grad,
    top,
    bottom,
    to_before,
    to_after,
    sums,
    ext,
    grad_flat,
    standard,
    inv_std,
    normed,
    branch_grad,
    hidden,
    active_grad,
    active,
    hidden_grad,
    up_sum,
    down_sum,
    bias_sum,
    tap_sums,
    row_sums,
    fields,
    mask,
    strips,
    weights,
    cotangent,
    up_weight,
    down_weight,
    done,
):
    ext_flat = ext.reshape(EXT_ROWS * EXT_COLS, LANES)
    rims = [strips.at[i] for i in range(len(STEPS))]
    copies = start_copies(
        (fields_hbm, mask_hbm, s0, s1, s2, s3, s4, s5)
        + (weights_hbm, cotangent_hbm, up_weight_hbm, down_weight_hbm),
        [fields, mask, *rims, weights, cotangent, up_weight, down_weight],
        done,
    )
    up_sum[...] = jnp.zeros_like(up_sum)
    down_sum[...] = jnp.zeros_like(down_sum)
    bias_sum[...] = jnp.zeros_like(bias_sum)
    tap_sums[...] = jnp.zeros_like(tap_sums)
    row_sums[...] = jnp.zeros_like(row_sums)
    for copy in copies[:2]:
        copy.wait()

    def centre(i, _):
        ext[HALO + i, pl.ds(8, TILE), :] = fields[i].astype(f32) * mask[i].astype(f32)
        return 0

    lax.fori_loop(0, TILE, centre, 0, unroll=4)
    for copy in copies[2:]:
        copy.wait()
    place_rims(ext, ext_flat, beside, where, rims)
    ones = jnp.ones((8, CELLS_IN_CHUNK), bf16)

    def chunk(step, _):
        first = pl.multiple_of(step * CHUNK, CHUNK)
        for g in range(GROUPS):
            values = conv_group(ext, weights, first, g)
            for row in range(CHUNK):
                standard[pl.ds(row * TILE + 8 * g, 8), :] = values[row]

        def normalise(row, _):
            cells = pl.ds(pl.multiple_of(row * TILE, TILE), TILE)
            conv = standard[cells, :]
            centered = conv - jnp.mean(conv, axis=-1, keepdims=True)
            inv = lax.rsqrt(jnp.mean(centered * centered, axis=-1, keepdims=True) + norm_eps)
            unit = centered * inv
            standard[cells, :] = unit
            inv_std[cells, :] = jnp.broadcast_to(inv, (TILE, LANES))
            normed[cells, :] = (unit * gain[...]).astype(bf16)
            weighted = mask[first + row].astype(f32) * scale[...]
            branch_grad[cells, :] = (weighted * cotangent[first + row].astype(f32)).astype(bf16)
            return 0

        lax.fori_loop(0, CHUNK, normalise, 0, unroll=CHUNK)
        hidden[...] = jnp.dot(normed[...], up_weight[...], preferred_element_type=f32)
        active_grad[...] = lax.dot_general(
            branch_grad[...],
            down_weight[...],
            (((1,), (1,)), ((), ())),
            preferred_element_type=f32,
        )

        def activate(i, _):
            cells = pl.ds(pl.multiple_of(i * 16, 16), 16)
            h = hidden[cells, :] + up_bias[...]
            t = pl.reciprocal(1.0 + TAIL_RATE * jnp.abs(h), approx=False)
            tail = TAIL_TERMS[-1] * t + TAIL_TERMS[-2]
            for term in TAIL_TERMS[-3::-1]:
                tail = tail * t + term
            bell = jnp.exp(-0.5 * h * h)
            tail = tail * t * bell
            phi = jnp.where(h >= 0, 1.0 - tail, tail)
            active[cells, :] = (h * phi).astype(bf16)
            slope = phi + h * (bell * inv_sqrt_two_pi)
            hidden_grad[cells, :] = (active_grad[cells, :] * slope).astype(bf16)
            return 0

        lax.fori_loop(0, CELLS_IN_CHUNK // 16, activate, 0, unroll=CELLS_IN_CHUNK // 16)
        hidden[:, 0:LANES] = jnp.dot(active[...], down_weight[...], preferred_element_type=f32)
        active_grad[:, 0:LANES] = lax.dot_general(
            hidden_grad[...], up_weight[...], (((1,), (1,)), ((), ())), preferred_element_type=f32
        )
        over_cells = (((0,), (0,)), ((), ()))
        down_sum[...] += lax.dot_general(
            branch_grad[...], active[...], over_cells, preferred_element_type=f32
        )
        up_sum[...] += lax.dot_general(
            normed[...], hidden_grad[...], over_cells, preferred_element_type=f32
        )
        bias_sum[...] += jnp.dot(ones, hidden_grad[...], preferred_element_type=f32)

        def finish(row, _):
            cells = pl.ds(pl.multiple_of(row * TILE, TILE), TILE)
            at = first + row
            masked_branch = mask[at].astype(f32) * hidden[cells, 0:LANES]
            block_out[at] = (fields[at].astype(f32) + masked_branch * scale[...]).astype(bf16)
            by_scale = masked_branch * cotangent[at].astype(f32)
            unit = standard[cells, :]
            grad = active_grad[cells, 0:LANES]
            by_gain = grad * unit
            u = grad * gain[...]
            mean_u = jnp.mean(u, axis=-1, keepdims=True)
            mean_us = jnp.mean(u * unit, axis=-1, keepdims=True)
            out = (inv_std[cells, :] * (u - mean_u - unit * mean_us)).astype(bf16)
            conv_grad[at] = out
            grad_flat[pl.ds(pl.multiple_of(at * TILE, TILE), TILE), :] = out.astype(f32)
            for k in range(GROUPS):
                row_sums[0:8, :] += by_scale[8 * k : 8 * k + 8]
                row_sums[8:16, :] += by_gain[8 * k : 8 * k + 8]
            return 0

        lax.fori_loop(0, CHUNK, finish, 0, unroll=CHUNK)
        for b in range(KERNEL):
            totals = [tap_sums[a * KERNEL + b] for a in range(KERNEL)]
            for g in range(GROUPS):
                grads = [
                    grad_flat[pl.ds((first + row) * TILE + 8 * g, 8), :] for row in range(CHUNK)
                ]
                column = PAD + 8 * g + DILATION * b
                for i in range(CHUNK + 2 * HALO):
                    window = ext[first + i, pl.ds(column, 8), :]
                    for a in range(KERNEL):
                        row = i - DILATION * a
                        if 0 <= row < CHUNK:
                            totals[a] = totals[a] + grads[row] * window
            for a in range(KERNEL):
                tap_sums[a * KERNEL + b] = totals[a]
        return 0

    lax.fori_loop(0, TILE // CHUNK, chunk, 0)
    pack_strips(grad_flat, beside, where, top, bottom, to_before, to_after)

    quarters = up_sum.shape[1] // LANES
    for q in range(quarters):
        lanes = slice(q * LANES, (q + 1) * LANES)
        sums[q * LANES : (q + 1) * LANES, :] = up_sum[:, lanes]
        sums[(quarters + q) * LANES : (quarters + q + 1) * LANES, :] = down_sum[:, lanes].T
    at = 2 * quarters * LANES
    sums[at:, :] = jnp.zeros((sums.shape[0] - at, LANES), f32)
    sums[at : at + TAPS, :] = jnp.sum(tap_sums[...], axis=1)
    sums[at + TAPS : at + TAPS + 1, :] = jnp.sum(row_sums[0:8, :], axis=0, keepdims=True)
    sums[at + TAPS + 1 : at + TAPS + 2, :] = jnp.sum(row_sums[8:16, :], axis=0, keepdims=True)
    for q in range(quarters):
        row = at + TAPS + 2 + q
        sums[row : row + 1, :] = bias_sum[0:1, q * LANES : (q + 1) * LANES]


def back_kernel(
    beside,
    where,
    conv_grad_hbm,
    s0,
    s1,
    s2,
    s3,
    s4,
    s5,
    weights_hbm,
    mask_hbm,
    cotangent_hbm,
    fields_grad,
    ext,
    conv_grad,
    strips,
    weights,
    mask,
    cotangent,
    done,
):
    ext_flat = ext.reshape(EXT_ROWS * EXT_COLS, LANES)
    rims = [strips.at[i] for i in range(len(STEPS))]
    copies = start_copies(
        (conv_grad_hbm, s0, s1, s2, s3, s4, s5, weights_hbm, mask_hbm, cotangent_hbm),
        [conv_grad, *rims, weights, mask, cotangent],
        done,
    )
    copies[0].wait()

    def centre(i, _):
        ext[HALO + i, pl.ds(8, TILE), :] = conv_grad[i].astype(f32)
        return 0

    lax.fori_loop(0, TILE, centre, 0, unroll=4)
    for copy in copies[1:]:
        copy.wait()
    place_rims(ext, ext_flat, beside, where, rims)

    def chunk(step, _):
        first = pl.multiple_of(step * CHUNK, CHUNK)
        columns = [conv_group(ext, weights, first, g, True) for g in range(GROUPS)]
        for row in range(CHUNK):
            at = first + row
            whole = jnp.concatenate([columns[g][row] for g in range(GROUPS)], axis=0)
            out = cotangent[at].astype(f32) + mask[at].astype(f32) * whole
            fields_grad[at] = out.astype(bf16)
        return 0

    lax.fori_loop(0, TILE // CHUNK, chunk, 0)


def unpack_kernel(total, kernel_grad, gain_grad, up_grad, bias_grad, down_grad, scale_grad):
    quarters = up_grad.shape[1] // LANES
    units = quarters * LANES
    for q in range(quarters):
        lanes = slice(q * LANES, (q + 1) * LANES)
        up_grad[:, lanes] = total[q * LANES : (q + 1) * LANES, :].astype(f32)
        down_grad[lanes, :] = total[units + q * LANES : units + (q + 1) * LANES, :].astype(f32)
    at = 2 * units
    rest = total[at : at + 64, :].astype(f32)
    for a in range(KERNEL):
        kernel_grad[a] = rest[a * KERNEL : (a + 1) * KERNEL]
    scale_grad[...] = rest[TAPS : TAPS + 1]
    gain_grad[...] = rest[TAPS + 1 : TAPS + 2]
    for q in range(quarters):
        row = TAPS + 2 + q
        bias_grad[:, q * LANES : (q + 1) * LANES] = rest[row : row + 1]


def shape(dims, dtype=bf16):
    return jax.ShapeDtypeStruct(dims, dtype)


STRIP = (HALO, TILE, LANES)
WHOLE = (TILE, TILE, LANES)


def call(kernel, scalars, operands, outs, scratch, flops, limit, spaces=VMEM):
    size = sum(math.prod(a.shape) * a.dtype.itemsize for a in (*operands, *outs))
    return pl.pallas_call(
        kernel,
        out_shape=outs,
        in_specs=[SMEM] * len(scalars) + (spaces if spaces is not VMEM else [VMEM] * len(operands)),
        out_specs=[VMEM] * len(outs),
        scratch_shapes=scratch,
        compiler_params=pltpu.CompilerParams(vmem_limit_bytes=limit),
        cost_estimate=pl.CostEstimate(flops=flops, bytes_accessed=size, transcendentals=0),
    )(*scalars, *operands)


def shifted(value, step):
    count = lax.axis_size(SPACE)
    first, last = (max(0, -step), min(count, count - step))
    return lax.ppermute(value, SPACE, [(source, source + step) for source in range(first, last)])


def exchange(top, bottom, to_before, to_after, steps=STEPS):
    sent = {3: bottom, 2: bottom, 1: to_after, -1: to_before, -2: top, -3: top}
    return {step: shifted(sent[-step], -step) for step in steps}


def spread(value, axes):
    copies = jnp.broadcast_to(value, (lax.axis_size(axes),) + value.shape)
    return lax.all_to_all(copies, axes, 0, 0, tiled=True)


def block_call(beside, where, *operands):
    units = operands[10].shape[1]
    quarters = units // LANES
    sum_rows = -(-(2 * units + TAPS + 2 + quarters) // SHARES) * SHARES
    return call(
        block_kernel,
        (beside, where),
        operands,
        [shape(WHOLE), shape(WHOLE)] + [shape(STRIP)] * 4 + [shape((sum_rows, LANES), f32)],
        [
            pltpu.VMEM((EXT_ROWS, EXT_COLS, LANES), f32),
            pltpu.VMEM((TILE * TILE, LANES), f32),
            pltpu.VMEM((CELLS_IN_CHUNK, LANES), f32),
            pltpu.VMEM((CELLS_IN_CHUNK, LANES), f32),
            pltpu.VMEM((CELLS_IN_CHUNK, LANES), bf16),
            pltpu.VMEM((CELLS_IN_CHUNK, LANES), bf16),
            pltpu.VMEM((CELLS_IN_CHUNK, units), f32),
            pltpu.VMEM((CELLS_IN_CHUNK, units), f32),
            pltpu.VMEM((CELLS_IN_CHUNK, units), bf16),
            pltpu.VMEM((CELLS_IN_CHUNK, units), bf16),
            pltpu.VMEM((LANES, units), f32),
            pltpu.VMEM((LANES, units), f32),
            pltpu.VMEM((8, units), f32),
            pltpu.VMEM((TAPS, 8, LANES), f32),
            pltpu.VMEM((16, LANES), f32),
            pltpu.VMEM(WHOLE, bf16),
            pltpu.VMEM(WHOLE, bf16),
            pltpu.VMEM((len(STEPS), *STRIP), bf16),
            pltpu.VMEM((KERNEL, KERNEL, LANES), f32),
            pltpu.VMEM(WHOLE, bf16),
            pltpu.VMEM((LANES, units), bf16),
            pltpu.VMEM((units, LANES), bf16),
            pltpu.SemaphoreType.DMA((12,)),
        ],
        12 * TILE * TILE * LANES * units,
        LARGE,
        [HBM] * 12 + [VMEM] * 3,
    )


def local(
    fields,
    cotangent,
    land_mask,
    neighbours,
    conv_kernel,
    norm_gain,
    up_weight,
    up_bias,
    down_weight,
    layer_scale,
):
    beside = neighbours
    where = lax.axis_index(SPACE).astype(jnp.int32)[None]
    tile, upstream = fields[0, 0], cotangent[0, 0]
    units = up_weight.shape[1]
    mask, *rims = call(
        pack_kernel,
        (beside, where),
        (land_mask, fields),
        [shape(WHOLE)] + [shape(STRIP)] * 4,
        [pltpu.VMEM((TILE * TILE, LANES), f32)],
        TILE * TILE * LANES,
        LARGE,
    )
    strips = exchange(*rims)
    strips = [strips[step] for step in STEPS]
    block_out, conv_grad, *rims, sums = block_call(
        beside,
        where,
        tile,
        mask,
        *strips,
        conv_kernel,
        upstream,
        up_weight,
        down_weight,
        norm_gain[None],
        up_bias[None],
        layer_scale[None],
    )
    sum_rows = sums.shape[0]
    cells = TILE * TILE * lax.axis_size(DP) * lax.axis_size(SPACE)
    part = sums.reshape(lax.axis_size(PLANE), -1, LANES)
    part = jnp.sum(lax.all_to_all(part, PLANE, 0, 0, tiled=True), axis=0)
    near = exchange(*rims, steps=(-2, -1, 1))
    part, rims, near = lax.optimization_barrier((part, rims, near))
    far = exchange(*rims, steps=(-3, 2, 3))
    part = jnp.sum(spread(part.astype(bf16), "z").astype(f32), axis=0) * (1.0 / math.sqrt(cells))
    part, far = lax.optimization_barrier((part, far))
    strips = [{**near, **far}[step] for step in STEPS]
    total = spread(part.astype(bf16), PLANE).reshape(sum_rows, LANES)
    (fields_grad,) = call(
        back_kernel,
        (beside, where),
        (conv_grad, *strips, conv_kernel, mask, upstream),
        [shape(WHOLE)],
        [
            pltpu.VMEM((EXT_ROWS, EXT_COLS, LANES), f32),
            pltpu.VMEM(WHOLE, bf16),
            pltpu.VMEM((len(STEPS), *STRIP), bf16),
            pltpu.VMEM((KERNEL, KERNEL, LANES), f32),
            pltpu.VMEM(WHOLE, bf16),
            pltpu.VMEM(WHOLE, bf16),
            pltpu.SemaphoreType.DMA((10,)),
        ],
        2 * TAPS * TILE * TILE * LANES,
        LARGE,
        [HBM] * 10,
    )
    total, fields_grad = lax.optimization_barrier((total, fields_grad))
    kernel_grad, gain_grad, up_grad, bias_grad, down_grad, scale_grad = call(
        unpack_kernel,
        (),
        (total,),
        [
            shape((KERNEL, KERNEL, LANES), f32),
            shape((1, LANES), f32),
            shape((LANES, units), f32),
            shape((1, units), f32),
            shape((units, LANES), f32),
            shape((1, LANES), f32),
        ],
        [],
        sum_rows * LANES,
        SMALL,
    )
    return (
        block_out[None, None],
        fields_grad[None, None],
        kernel_grad,
        gain_grad[0],
        up_grad,
        bias_grad[0],
        down_grad,
        scale_grad[0],
    )


def solution(mesh):
    fine = jax.sharding.Mesh(mesh.devices.reshape(2, 4, 2, 16, 2), DP + SPACE)
    tiles = P(DP, SPACE, None, None, None)
    return jax.shard_map(
        local,
        mesh=fine,
        in_specs=(
            tiles,
            tiles,
            P(SPACE, None, None),
            P(SPACE, None),
            P(),
            P(),
            P(),
            P(),
            P(),
            P(),
        ),
        out_specs=(tiles, tiles, P(), P(), P(), P(), P(), P()),
        check_vma=False,
    )
```

```python
import math

import jax
import jax.numpy as jnp
from jax import lax
from jax.experimental import pallas as pl
from jax.experimental.pallas import tpu as pltpu
from jax.sharding import PartitionSpec as P

KERNEL = 7
DILATION = 2
HALO = 6
TAPS = KERNEL * KERNEL
TILE = 48
LANES = 128
PAD = 2
EXT_ROWS = TILE + 2 * HALO
EXT_COLS = 64
CHUNK = 16
CELLS_IN_CHUNK = CHUNK * TILE
GROUPS = TILE // 8
STEPS = (-3, -2, -1, 1, 2, 3)
LARGE, SMALL = 60 * 2**20, 16 * 2**20
DP = ("x_hi", "y", "core")
SPACE = ("z", "x_lo")
PLANE = ("x_hi", "y", "core", "x_lo")

SHARES = 32 * 8

norm_eps = 1e-06
inv_sqrt_two_pi = 0.3989422804014327
TAIL_RATE = 0.3889087296526013
TAIL_TERMS = (
    0.15079174476614957,
    0.19542085643011212,
    -0.02071252121020706,
    0.379856419408137,
    -0.25901857729927547,
    0.05366208632016299,
)

f32 = jnp.float32
bf16 = jnp.bfloat16
VMEM = pl.BlockSpec(memory_space=pltpu.VMEM)
SMEM = pl.BlockSpec(memory_space=pltpu.SMEM)
HBM = pl.BlockSpec(memory_space=pltpu.HBM)


def pack_strips(flat, beside, where, top, bottom, to_before, to_after):
    position = where[0]
    upper = flat[0 : HALO * TILE, :].astype(bf16).reshape(HALO, TILE, LANES)
    lower = flat[(TILE - HALO) * TILE :, :].astype(bf16).reshape(HALO, TILE, LANES)
    top[...] = upper
    bottom[...] = lower
    to_before[...] = upper
    to_after[...] = lower

    def columns(out, first):
        for c in range(HALO):
            parts = [
                flat[pl.ds(8 * g * TILE + first + c, 8, stride=TILE), :] for g in range(GROUPS)
            ]
            out[c] = jnp.concatenate(parts, axis=0).astype(bf16)

    for out, step in ((to_before, -1), (to_after, 1)):
        for direction, first in ((2, 0), (3, TILE - HALO)):
            source = beside[0, direction]

            @pl.when((source >= 0) & (source - position == step))
            def _(out=out, first=first):
                columns(out, first)


def place_rims(ext, ext_flat, beside, where, strips):
    position = where[0]
    zero_rows = jnp.zeros((HALO, EXT_COLS, LANES), f32)
    zero_cols = jnp.zeros((TILE, 8, LANES), f32)
    ext[0:HALO] = zero_rows
    ext[HALO + TILE :] = zero_rows
    ext[HALO : HALO + TILE, 0:8, :] = zero_cols
    ext[HALO : HALO + TILE, 8 + TILE :, :] = zero_cols
    last = TILE - 8

    def put_rows(first):
        def put(strip):
            ext[first : first + HALO, 8 : 8 + TILE, :] = strip.astype(f32)

        return put

    def put_corner(first, east):
        def put(strip):
            wide = strip.astype(f32)
            if east:
                ext[first : first + HALO, 8 + TILE :, :] = wide[:, 0:8]
            else:
                ext[first : first + HALO, 0:8, :] = wide[:, last:]

        return put

    def put_columns(first):
        def put(strip):
            wide = strip.astype(f32)
            for c in range(HALO):
                for g in range(GROUPS):
                    at = (HALO + 8 * g) * EXT_COLS + first + c
                    ext_flat[pl.ds(at, 8, stride=EXT_COLS), :] = wide[c, 8 * g : 8 * g + 8]

        return put

    south_row = HALO + TILE
    before, after = (-1, -2, -3), (1, 2, 3)
    for direction, steps, put in (
        (4, before, put_corner(0, False)),
        (5, before, put_corner(0, True)),
        (6, after, put_corner(south_row, False)),
        (7, after, put_corner(south_row, True)),
        (0, before, put_rows(0)),
        (1, after, put_rows(south_row)),
        (2, (-1, 1), put_columns(PAD)),
        (3, (-1, 1), put_columns(8 + TILE)),
    ):
        source = beside[0, direction]
        for step in steps:

            @pl.when((source >= 0) & (source - position == step))
            def _(step=step, put=put):
                put(strips[STEPS.index(step)][...])


def conv_group(ext, weights, first_row, g, reverse=False):
    def tap(a, b):
        return (KERNEL - 1 - a, KERNEL - 1 - b) if reverse else (a, b)

    sums = [None] * CHUNK
    for b in range(KERNEL):
        taps = [
            jnp.broadcast_to(weights[tap(a, b)[0], pl.ds(tap(a, b)[1], 1), :], (8, LANES))
            for a in range(KERNEL)
        ]
        column = PAD + 8 * g + DILATION * b
        for i in range(CHUNK + 2 * HALO):
            window = ext[first_row + i, pl.ds(column, 8), :]
            for a in range(KERNEL):
                row = i - DILATION * a
                if 0 <= row < CHUNK:
                    term = taps[a] * window
                    sums[row] = term if sums[row] is None else sums[row] + term
    return sums


def pack_kernel(beside, where, land_mask, fields, mask, top, bottom, to_before, to_after, flat):
    side = (TILE, TILE)
    diagonal = lax.broadcasted_iota(jnp.int32, side, 0) == lax.broadcasted_iota(jnp.int32, side, 1)
    by_column = lax.dot_general(
        land_mask[0].astype(f32).astype(bf16),
        jnp.where(diagonal, 1.0, 0.0).astype(bf16),
        (((0,), (0,)), ((), ())),
        preferred_element_type=f32,
    )
    for row in range(TILE):
        wide = jnp.broadcast_to(by_column[:, row : row + 1], (TILE, LANES))
        mask[row] = wide.astype(bf16)
        flat[row * TILE : (row + 1) * TILE, :] = fields[0, 0, row].astype(f32) * wide
    pack_strips(flat, beside, where, top, bottom, to_before, to_after)


def start_copies(sources, targets, done):
    copies = [
        pltpu.make_async_copy(source, target, done.at[i])
        for i, (source, target) in enumerate(zip(sources, targets))
    ]
    for copy in copies:
        copy.start()
    return copies


def block_kernel(
    beside,
    where,
    fields_hbm,
    mask_hbm,
    s0,
    s1,
    s2,
    s3,
    s4,
    s5,
    weights_hbm,
    cotangent_hbm,
    up_weight_hbm,
    down_weight_hbm,
    gain,
    up_bias,
    scale,
    block_out,
    conv_grad,
    top,
    bottom,
    to_before,
    to_after,
    sums,
    ext,
    grad_flat,
    standard,
    inv_std,
    normed,
    branch_grad,
    hidden,
    active_grad,
    active,
    hidden_grad,
    up_sum,
    down_sum,
    bias_sum,
    tap_sums,
    row_sums,
    fields,
    mask,
    strips,
    weights,
    cotangent,
    up_weight,
    down_weight,
    done,
):
    ext_flat = ext.reshape(EXT_ROWS * EXT_COLS, LANES)
    rims = [strips.at[i] for i in range(len(STEPS))]
    copies = start_copies(
        (fields_hbm, mask_hbm, s0, s1, s2, s3, s4, s5)
        + (weights_hbm, cotangent_hbm, up_weight_hbm, down_weight_hbm),
        [fields, mask, *rims, weights, cotangent, up_weight, down_weight],
        done,
    )
    up_sum[...] = jnp.zeros_like(up_sum)
    down_sum[...] = jnp.zeros_like(down_sum)
    bias_sum[...] = jnp.zeros_like(bias_sum)
    tap_sums[...] = jnp.zeros_like(tap_sums)
    row_sums[...] = jnp.zeros_like(row_sums)
    for copy in copies[:2]:
        copy.wait()

    def centre(i, _):
        ext[HALO + i, pl.ds(8, TILE), :] = fields[i].astype(f32) * mask[i].astype(f32)
        return 0

    lax.fori_loop(0, TILE, centre, 0, unroll=4)
    for copy in copies[2:8]:
        copy.wait()
    place_rims(ext, ext_flat, beside, where, rims)
    for copy in copies[8:]:
        copy.wait()
    ones = jnp.ones((8, CELLS_IN_CHUNK), bf16)

    def chunk(step, _):
        first = pl.multiple_of(step * CHUNK, CHUNK)
        for g in range(GROUPS):
            values = conv_group(ext, weights, first, g)
            for row in range(CHUNK):
                standard[pl.ds(row * TILE + 8 * g, 8), :] = values[row]

        def normalise(row, _):
            cells = pl.ds(pl.multiple_of(row * TILE, TILE), TILE)
            conv = standard[cells, :]
            centered = conv - jnp.mean(conv, axis=-1, keepdims=True)
            inv = lax.rsqrt(jnp.mean(centered * centered, axis=-1, keepdims=True) + norm_eps)
            unit = centered * inv
            standard[cells, :] = unit
            inv_std[cells, :] = jnp.broadcast_to(inv, (TILE, LANES))
            normed[cells, :] = (unit * gain[...]).astype(bf16)
            weighted = mask[first + row].astype(f32) * scale[...]
            branch_grad[cells, :] = (weighted * cotangent[first + row].astype(f32)).astype(bf16)
            return 0

        lax.fori_loop(0, CHUNK, normalise, 0, unroll=CHUNK)
        hidden[...] = jnp.dot(normed[...], up_weight[...], preferred_element_type=f32)
        active_grad[...] = lax.dot_general(
            branch_grad[...],
            down_weight[...],
            (((1,), (1,)), ((), ())),
            preferred_element_type=f32,
        )

        def activate(i, _):
            cells = pl.ds(pl.multiple_of(i * 16, 16), 16)
            h = hidden[cells, :] + up_bias[...]
            t = pl.reciprocal(1.0 + TAIL_RATE * jnp.abs(h), approx=False)
            tail = TAIL_TERMS[-1] * t + TAIL_TERMS[-2]
            for term in TAIL_TERMS[-3::-1]:
                tail = tail * t + term
            bell = jnp.exp(-0.5 * h * h)
            tail = tail * t * bell
            phi = jnp.where(h >= 0, 1.0 - tail, tail)
            active[cells, :] = (h * phi).astype(bf16)
            slope = phi + h * (bell * inv_sqrt_two_pi)
            hidden_grad[cells, :] = (active_grad[cells, :] * slope).astype(bf16)
            return 0

        lax.fori_loop(0, CELLS_IN_CHUNK // 16, activate, 0, unroll=CELLS_IN_CHUNK // 16)
        hidden[:, 0:LANES] = jnp.dot(active[...], down_weight[...], preferred_element_type=f32)
        active_grad[:, 0:LANES] = lax.dot_general(
            hidden_grad[...], up_weight[...], (((1,), (1,)), ((), ())), preferred_element_type=f32
        )
        over_cells = (((0,), (0,)), ((), ()))
        down_sum[...] += lax.dot_general(
            branch_grad[...], active[...], over_cells, preferred_element_type=f32
        )
        up_sum[...] += lax.dot_general(
            normed[...], hidden_grad[...], over_cells, preferred_element_type=f32
        )
        bias_sum[...] += jnp.dot(ones, hidden_grad[...], preferred_element_type=f32)

        def finish(row, _):
            cells = pl.ds(pl.multiple_of(row * TILE, TILE), TILE)
            at = first + row
            masked_branch = mask[at].astype(f32) * hidden[cells, 0:LANES]
            block_out[at] = (fields[at].astype(f32) + masked_branch * scale[...]).astype(bf16)
            by_scale = masked_branch * cotangent[at].astype(f32)
            unit = standard[cells, :]
            grad = active_grad[cells, 0:LANES]
            by_gain = grad * unit
            u = grad * gain[...]
            mean_u = jnp.mean(u, axis=-1, keepdims=True)
            mean_us = jnp.mean(u * unit, axis=-1, keepdims=True)
            out = (inv_std[cells, :] * (u - mean_u - unit * mean_us)).astype(bf16)
            conv_grad[at] = out
            grad_flat[pl.ds(pl.multiple_of(at * TILE, TILE), TILE), :] = out.astype(f32)
            for k in range(GROUPS):
                row_sums[0:8, :] += by_scale[8 * k : 8 * k + 8]
                row_sums[8:16, :] += by_gain[8 * k : 8 * k + 8]
            return 0

        lax.fori_loop(0, CHUNK, finish, 0, unroll=CHUNK)
        for b in range(KERNEL):
            totals = [tap_sums[a * KERNEL + b] for a in range(KERNEL)]
            for g in range(GROUPS):
                grads = [
                    grad_flat[pl.ds((first + row) * TILE + 8 * g, 8), :] for row in range(CHUNK)
                ]
                column = PAD + 8 * g + DILATION * b
                for i in range(CHUNK + 2 * HALO):
                    window = ext[first + i, pl.ds(column, 8), :]
                    for a in range(KERNEL):
                        row = i - DILATION * a
                        if 0 <= row < CHUNK:
                            totals[a] = totals[a] + grads[row] * window
            for a in range(KERNEL):
                tap_sums[a * KERNEL + b] = totals[a]
        return 0

    lax.fori_loop(0, TILE // CHUNK, chunk, 0)
    pack_strips(grad_flat, beside, where, top, bottom, to_before, to_after)

    quarters = up_sum.shape[1] // LANES
    for q in range(quarters):
        lanes = slice(q * LANES, (q + 1) * LANES)
        sums[q * LANES : (q + 1) * LANES, :] = up_sum[:, lanes]
        sums[(quarters + q) * LANES : (quarters + q + 1) * LANES, :] = down_sum[:, lanes].T
    at = 2 * quarters * LANES
    sums[at:, :] = jnp.zeros((sums.shape[0] - at, LANES), f32)
    sums[at : at + TAPS, :] = jnp.sum(tap_sums[...], axis=1)
    sums[at + TAPS : at + TAPS + 1, :] = jnp.sum(row_sums[0:8, :], axis=0, keepdims=True)
    sums[at + TAPS + 1 : at + TAPS + 2, :] = jnp.sum(row_sums[8:16, :], axis=0, keepdims=True)
    for q in range(quarters):
        row = at + TAPS + 2 + q
        sums[row : row + 1, :] = bias_sum[0:1, q * LANES : (q + 1) * LANES]


def back_kernel(
    beside,
    where,
    conv_grad_hbm,
    s0,
    s1,
    s2,
    s3,
    s4,
    s5,
    weights_hbm,
    mask_hbm,
    cotangent_hbm,
    fields_grad,
    ext,
    conv_grad,
    strips,
    weights,
    mask,
    cotangent,
    done,
):
    ext_flat = ext.reshape(EXT_ROWS * EXT_COLS, LANES)
    rims = [strips.at[i] for i in range(len(STEPS))]
    copies = start_copies(
        (conv_grad_hbm, s0, s1, s2, s3, s4, s5, weights_hbm, mask_hbm, cotangent_hbm),
        [conv_grad, *rims, weights, mask, cotangent],
        done,
    )
    copies[0].wait()

    def centre(i, _):
        ext[HALO + i, pl.ds(8, TILE), :] = conv_grad[i].astype(f32)
        return 0

    lax.fori_loop(0, TILE, centre, 0, unroll=4)
    for copy in copies[1:7]:
        copy.wait()
    place_rims(ext, ext_flat, beside, where, rims)
    for copy in copies[7:]:
        copy.wait()

    def chunk(step, _):
        first = pl.multiple_of(step * CHUNK, CHUNK)
        columns = [conv_group(ext, weights, first, g, True) for g in range(GROUPS)]
        for row in range(CHUNK):
            at = first + row
            whole = jnp.concatenate([columns[g][row] for g in range(GROUPS)], axis=0)
            out = cotangent[at].astype(f32) + mask[at].astype(f32) * whole
            fields_grad[at] = out.astype(bf16)
        return 0

    lax.fori_loop(0, TILE // CHUNK, chunk, 0)


def unpack_kernel(total, kernel_grad, gain_grad, up_grad, bias_grad, down_grad, scale_grad):
    quarters = up_grad.shape[1] // LANES
    units = quarters * LANES
    for q in range(quarters):
        lanes = slice(q * LANES, (q + 1) * LANES)
        up_grad[:, lanes] = total[q * LANES : (q + 1) * LANES, :].astype(f32)
        down_grad[lanes, :] = total[units + q * LANES : units + (q + 1) * LANES, :].astype(f32)
    at = 2 * units
    rest = total[at : at + 64, :].astype(f32)
    for a in range(KERNEL):
        kernel_grad[a] = rest[a * KERNEL : (a + 1) * KERNEL]
    scale_grad[...] = rest[TAPS : TAPS + 1]
    gain_grad[...] = rest[TAPS + 1 : TAPS + 2]
    for q in range(quarters):
        row = TAPS + 2 + q
        bias_grad[:, q * LANES : (q + 1) * LANES] = rest[row : row + 1]


def shape(dims, dtype=bf16):
    return jax.ShapeDtypeStruct(dims, dtype)


STRIP = (HALO, TILE, LANES)
WHOLE = (TILE, TILE, LANES)


def call(kernel, scalars, operands, outs, scratch, flops, limit, spaces=VMEM):
    size = sum(math.prod(a.shape) * a.dtype.itemsize for a in (*operands, *outs))
    return pl.pallas_call(
        kernel,
        out_shape=outs,
        in_specs=[SMEM] * len(scalars) + (spaces if spaces is not VMEM else [VMEM] * len(operands)),
        out_specs=[VMEM] * len(outs),
        scratch_shapes=scratch,
        compiler_params=pltpu.CompilerParams(vmem_limit_bytes=limit),
        cost_estimate=pl.CostEstimate(flops=flops, bytes_accessed=size, transcendentals=0),
    )(*scalars, *operands)


def shifted(value, step):
    count = lax.axis_size(SPACE)
    first, last = (max(0, -step), min(count, count - step))
    return lax.ppermute(value, SPACE, [(source, source + step) for source in range(first, last)])


def exchange(top, bottom, to_before, to_after, steps=STEPS):
    sent = {3: bottom, 2: bottom, 1: to_after, -1: to_before, -2: top, -3: top}
    return {step: shifted(sent[-step], -step) for step in steps}


def spread(value, axes):
    copies = jnp.broadcast_to(value, (lax.axis_size(axes),) + value.shape)
    return lax.all_to_all(copies, axes, 0, 0, tiled=True)


def block_call(beside, where, *operands):
    units = operands[10].shape[1]
    quarters = units // LANES
    sum_rows = -(-(2 * units + TAPS + 2 + quarters) // SHARES) * SHARES
    return call(
        block_kernel,
        (beside, where),
        operands,
        [shape(WHOLE), shape(WHOLE)] + [shape(STRIP)] * 4 + [shape((sum_rows, LANES), f32)],
        [
            pltpu.VMEM((EXT_ROWS, EXT_COLS, LANES), f32),
            pltpu.VMEM((TILE * TILE, LANES), f32),
            pltpu.VMEM((CELLS_IN_CHUNK, LANES), f32),
            pltpu.VMEM((CELLS_IN_CHUNK, LANES), f32),
            pltpu.VMEM((CELLS_IN_CHUNK, LANES), bf16),
            pltpu.VMEM((CELLS_IN_CHUNK, LANES), bf16),
            pltpu.VMEM((CELLS_IN_CHUNK, units), f32),
            pltpu.VMEM((CELLS_IN_CHUNK, units), f32),
            pltpu.VMEM((CELLS_IN_CHUNK, units), bf16),
            pltpu.VMEM((CELLS_IN_CHUNK, units), bf16),
            pltpu.VMEM((LANES, units), f32),
            pltpu.VMEM((LANES, units), f32),
            pltpu.VMEM((8, units), f32),
            pltpu.VMEM((TAPS, 8, LANES), f32),
            pltpu.VMEM((16, LANES), f32),
            pltpu.VMEM(WHOLE, bf16),
            pltpu.VMEM(WHOLE, bf16),
            pltpu.VMEM((len(STEPS), *STRIP), bf16),
            pltpu.VMEM((KERNEL, KERNEL, LANES), f32),
            pltpu.VMEM(WHOLE, bf16),
            pltpu.VMEM((LANES, units), bf16),
            pltpu.VMEM((units, LANES), bf16),
            pltpu.SemaphoreType.DMA((12,)),
        ],
        12 * TILE * TILE * LANES * units,
        LARGE,
        [HBM] * 12 + [VMEM] * 3,
    )


def local(
    fields,
    cotangent,
    land_mask,
    neighbours,
    conv_kernel,
    norm_gain,
    up_weight,
    up_bias,
    down_weight,
    layer_scale,
):
    beside = neighbours
    where = lax.axis_index(SPACE).astype(jnp.int32)[None]
    tile, upstream = fields[0, 0], cotangent[0, 0]
    units = up_weight.shape[1]
    mask, *rims = call(
        pack_kernel,
        (beside, where),
        (land_mask, fields),
        [shape(WHOLE)] + [shape(STRIP)] * 4,
        [pltpu.VMEM((TILE * TILE, LANES), f32)],
        TILE * TILE * LANES,
        LARGE,
    )
    strips = exchange(*rims)
    strips = [strips[step] for step in STEPS]
    block_out, conv_grad, *rims, sums = block_call(
        beside,
        where,
        tile,
        mask,
        *strips,
        conv_kernel,
        upstream,
        up_weight,
        down_weight,
        norm_gain[None],
        up_bias[None],
        layer_scale[None],
    )
    sum_rows = sums.shape[0]
    cells = TILE * TILE * lax.axis_size(DP) * lax.axis_size(SPACE)
    part = sums.reshape(lax.axis_size(PLANE), -1, LANES)
    part = jnp.sum(lax.all_to_all(part, PLANE, 0, 0, tiled=True), axis=0)
    near = exchange(*rims, steps=(-2, -1, 1, 2))
    part, rims, near = lax.optimization_barrier((part, rims, near))
    far = exchange(*rims, steps=(-3, 3))
    part = jnp.sum(spread(part.astype(bf16), "z").astype(f32), axis=0) * (1.0 / math.sqrt(cells))
    part, far = lax.optimization_barrier((part, far))
    strips = [{**near, **far}[step] for step in STEPS]
    total = spread(part.astype(bf16), PLANE).reshape(sum_rows, LANES)
    (fields_grad,) = call(
        back_kernel,
        (beside, where),
        (conv_grad, *strips, conv_kernel, mask, upstream),
        [shape(WHOLE)],
        [
            pltpu.VMEM((EXT_ROWS, EXT_COLS, LANES), f32),
            pltpu.VMEM(WHOLE, bf16),
            pltpu.VMEM((len(STEPS), *STRIP), bf16),
            pltpu.VMEM((KERNEL, KERNEL, LANES), f32),
            pltpu.VMEM(WHOLE, bf16),
            pltpu.VMEM(WHOLE, bf16),
            pltpu.SemaphoreType.DMA((10,)),
        ],
        2 * TAPS * TILE * TILE * LANES,
        LARGE,
        [HBM] * 10,
    )
    total, fields_grad = lax.optimization_barrier((total, fields_grad))
    kernel_grad, gain_grad, up_grad, bias_grad, down_grad, scale_grad = call(
        unpack_kernel,
        (),
        (total,),
        [
            shape((KERNEL, KERNEL, LANES), f32),
            shape((1, LANES), f32),
            shape((LANES, units), f32),
            shape((1, units), f32),
            shape((units, LANES), f32),
            shape((1, LANES), f32),
        ],
        [],
        sum_rows * LANES,
        SMALL,
    )
    return (
        block_out[None, None],
        fields_grad[None, None],
        kernel_grad,
        gain_grad[0],
        up_grad,
        bias_grad[0],
        down_grad,
        scale_grad[0],
    )


def solution(mesh):
    fine = jax.sharding.Mesh(mesh.devices.reshape(2, 4, 2, 16, 2), DP + SPACE)
    tiles = P(DP, SPACE, None, None, None)
    return jax.shard_map(
        local,
        mesh=fine,
        in_specs=(
            tiles,
            tiles,
            P(SPACE, None, None),
            P(SPACE, None),
            P(),
            P(),
            P(),
            P(),
            P(),
            P(),
        ),
        out_specs=(tiles, tiles, P(), P(), P(), P(), P(), P()),
        check_vma=False,
    )
```
